256 devices in a mesh: dp: 16 (over z_hi, y), ctx: 16 (over x, z_lo, core).
Axes of the slice: x: 4, y: 4, z: 8 (z_hi: 4, z_lo: 2; z = z_hi * 2 + z_lo), core: 2. Of those that a mesh axis runs over, the one named last changes fastest.
Arguments:
- value_in: float32 [16, 128, 4096], P('dp', None, 'ctx'), may hold values from -6 to 6
- key_in: float32 [16, 128, 4096], P('dp', None, 'ctx'), may hold values from -6 to 6
- query_in: float32 [16, 128, 4096], P('dp', None, 'ctx'), may hold values from -6 to 6
- cotangent: float32 [16, 128, 4096], P('dp', None, 'ctx'), may hold values from -6 to 6
- filter_param: float32 [128, 4096], P(None, 'ctx'), may hold values from -6 to 6
Outputs:
- query_grad: float32 [16, 128, 4096], P('dp', None, 'ctx')
- key_grad: float32 [16, 128, 4096], P('dp', None, 'ctx')
- value_grad: float32 [16, 128, 4096], P('dp', None, 'ctx')
- filter_grad: float32 [128, 4096], P(None, 'ctx')
The draws below stay inside these ranges and needn't reach their ends.
All inputs are finite; a program needn't handle non-finite values.
Results may differ from the reference program's by a relative error of at most 0.0003.
Values sent between devices are 32-bit elements; how exact they have to be, the bound alone decides.
No kernel may reach another device: no remote copies, remote signals or barrier semaphores. Data moves between devices by JAX's collectives and lax.ppermute only.
A program may use at most 64 MiB of HBM per device.

```python
import math
import jax
import jax.numpy as jnp
from jax import lax

C = 128
LENGTH = 4096
SEQS = 16


def shard_levels(key, shape, shards, low, high):
    gain = 1.0
    for dim, parts in shards:
        steps = jax.random.uniform(jax.random.fold_in(jax.random.fold_in(key, 6), dim), (parts,), jnp.float32, low / len(shards), high / len(shards))
        gain = gain * jnp.repeat(jnp.exp(steps), shape[dim] // parts).reshape((-1,) + (1,) * (len(shape) - 1 - dim))
    return gain


def centred(stream_key, extent, spread, bound, pieces=(), held_as=jnp.bfloat16):
    factor_of = shard_levels(stream_key, extent, pieces, -0.22, 0.18) if pieces else 1.0
    result = jax.random.normal(stream_key, extent, jnp.float32) * spread * factor_of
    return jnp.minimum(jnp.maximum(result, -bound), bound).astype(held_as)


def setup_inputs(seed: int = 0) -> dict:
    key_list = jax.random.split(jax.random.key(seed), 6)
    value_in = centred(key_list[0], (SEQS, C, LENGTH), 1.0, 6.0, ((0, 16), (2, 16)), jnp.float32)
    key_in = centred(key_list[1], (SEQS, C, LENGTH), 1.0, 6.0, ((0, 16), (2, 16)), jnp.float32)
    query_in = centred(key_list[2], (SEQS, C, LENGTH), 1.0, 6.0, ((0, 16), (2, 16)), jnp.float32)
    cotangent = centred(key_list[3], (SEQS, C, LENGTH), 1.0, 6.0, ((0, 16), (2, 16)), jnp.float32)
    filter_param = centred(key_list[4], (C, LENGTH), 1.0, 6.0, ((1, 16),), jnp.float32)
    return dict(value_in=value_in, key_in=key_in, query_in=query_in, cotangent=cotangent, filter_param=filter_param)


def reference(value_in, key_in, query_in, cotangent, filter_param):
    padded = 2 * LENGTH
    scale = 1.0 / math.sqrt(LENGTH)
    gated = key_in * value_in
    taps = filter_param * scale
    weight_grad = cotangent * query_in
    taps_spec = jnp.fft.rfft(taps, n=padded)
    gated_spec = jnp.fft.rfft(gated, n=padded)
    weight_spec = jnp.fft.rfft(weight_grad, n=padded)
    conv = jnp.fft.irfft(gated_spec * taps_spec[None], n=padded)[..., :LENGTH]
    gated_grad = jnp.fft.irfft(weight_spec * jnp.conj(taps_spec)[None], n=padded)[..., :LENGTH]
    summed = lax.optimization_barrier(jnp.sum(weight_spec * jnp.conj(gated_spec), axis=0))
    filter_grad = jnp.fft.irfft(summed, n=padded)[..., :LENGTH] * scale
    query_grad = cotangent * conv
    key_grad = gated_grad * value_in
    value_grad = gated_grad * key_in
    return (query_grad, key_grad, value_grad, filter_grad)
```

```python
import math

import jax
import jax.numpy as jnp
import numpy as np
from jax import lax
from jax.experimental import pallas as pl
from jax.experimental.pallas import tpu as pltpu
from jax.sharding import Mesh, PartitionSpec as P

AXES = ("zh", "y", "x", "zl", "core")
FAR = ("y", "x", "zl", "core")
BLOCKS = 17
CLASSES = [0, 16, 8, 4, 20] + [8 * j + 2 for j in range(4)] + [4 * j + 1 for j in range(8)]
VMEM = pl.BlockSpec(memory_space=pltpu.VMEM)
HBM = pl.BlockSpec(memory_space=pltpu.HBM)
PARAMS = pltpu.CompilerParams(vmem_limit_bytes=48 * 1024 * 1024)


def tables():
    lane = np.arange(128)
    forward = np.zeros((256, 256))
    angle = 2 * np.pi * np.outer(lane, lane) / 128
    c, s = np.cos(angle), np.sin(angle)
    forward = np.block([[c, -s], [s, c]])
    inverse = np.block([[c, s], [-s, c]]) * (2.0 / 8192)

    def split(table):
        high = table.astype(np.float32).astype(jnp.bfloat16)
        low = (table - high.astype(np.float64)).astype(np.float32).astype(jnp.bfloat16)
        return np.concatenate([high, low], 0)

    row_half = np.arange(8) // 4
    twiddle = np.zeros((BLOCKS, 2, 8, 128), np.float32)
    rowfix = np.zeros((BLOCKS, 2, 8, 128), np.float32)
    for index, k in enumerate(CLASSES):
        angle = -2 * np.pi * np.outer(k + 32 * row_half, lane) / 8192
        twiddle[index, 0], twiddle[index, 1] = np.cos(angle), np.sin(angle)
        angle = np.repeat((-2 * np.pi * k * row_half / 64)[:, None], 128, 1)
        rowfix[index, 0], rowfix[index, 1] = np.cos(angle), np.sin(angle)
    return split(forward), split(inverse), twiddle, rowfix


def add(a, b):
    return (a[0] + b[0], a[1] + b[1])


def sub(a, b):
    return (a[0] - b[0], a[1] - b[1])


def turn(a, step, period, sign):
    step = step % period
    if step == 0:
        return a
    if 4 * step == period:
        return (-a[1], a[0]) if sign > 0 else (a[1], -a[0])
    if 8 * step == period:
        r = np.float32(math.sqrt(0.5))
        if sign > 0:
            return ((a[0] - a[1]) * r, (a[0] + a[1]) * r)
        return ((a[0] + a[1]) * r, (a[1] - a[0]) * r)
    angle = sign * 2 * math.pi * step / period
    c, s = np.float32(math.cos(angle)), np.float32(math.sin(angle))
    return (a[0] * c - a[1] * s, a[0] * s + a[1] * c)


def small_dft(z, sign):
    n = len(z)
    if n == 1:
        return z
    even, odd = small_dft(z[0::2], sign), small_dft(z[1::2], sign)
    odd = [turn(value, j, n, sign) for j, value in enumerate(odd)]
    return [add(a, b) for a, b in zip(even, odd)] + [sub(a, b) for a, b in zip(even, odd)]


def blocks_forward(x):
    v = [x[c] + x[c + 8] for c in range(8)]
    u = [x[c] - x[c + 8] for c in range(8)]
    odd = small_dft([turn((x[c], -x[c + 8]), c, 32, -1) for c in range(8)], -1)
    two = small_dft([turn((u[c], -u[c + 4]), c, 16, -1) for c in range(4)], -1)
    a = [v[c] + v[c + 4] for c in range(4)]
    b = [v[c] - v[c + 4] for c in range(4)]
    four = small_dft([turn((b[c], -b[c + 2]), c, 8, -1) for c in range(2)], -1)
    e, o = a[0] + a[2], a[1] + a[3]
    eight = (a[0] - a[2], a[3] - a[1])
    return [(e + o, None), (e - o, None), eight] + four + two + odd


def blocks_inverse(spectrum):
    zero, sixteen, eight = spectrum[0], spectrum[1], spectrum[2]
    four, two, odd = spectrum[3:5], spectrum[5:9], spectrum[9:17]
    e, o = (zero[0] + sixteen[0]) * 0.5, (zero[0] - sixteen[0]) * 0.5
    a = [e + eight[0], o - eight[1], e - eight[0], o + eight[1]]
    g = [turn(value, c, 8, 1) for c, value in enumerate(small_dft(four, 1))]
    b = [g[0][0], g[1][0], -g[0][1], -g[1][1]]
    v = [a[c] + b[c] for c in range(4)] + [a[c] - b[c] for c in range(4)]
    g = [turn(value, c, 16, 1) for c, value in enumerate(small_dft(two, 1))]
    u = [value[0] for value in g] + [-value[1] for value in g]
    g = [turn(value, c, 32, 1) for c, value in enumerate(small_dft(odd, 1))]
    p = [v[c] + u[c] for c in range(8)]
    m = [v[c] - u[c] for c in range(8)]
    return [p[c] + g[c][0] for c in range(8)] + [m[c] - g[c][1] for c in range(8)]


def half_sign():
    rows = lax.broadcasted_iota(jnp.int32, (8, 128), 0)
    return jnp.where(rows < 4, 1.0, -1.0).astype(jnp.float32)


def swap_halves(a):
    return pltpu.roll(a, 4, 0)


def times(a, b, conjugate=False):
    if conjugate:
        return (a[0] * b[0] + a[1] * b[1], a[1] * b[0] - a[0] * b[1])
    return (a[0] * b[0] - a[1] * b[1], a[0] * b[1] + a[1] * b[0])


def butterfly(a, sign):
    return (a[0] * sign + swap_halves(a[0]), a[1] * sign + swap_halves(a[1]))


def multiply(source, target, table, rows, step):
    high_table, low_table = table[0:256, :], table[256:512, :]
    for start in range(0, rows, step):
        block = source[start : start + step, :]
        high = block.astype(jnp.bfloat16)
        low = (block - high.astype(jnp.float32)).astype(jnp.bfloat16)
        total = jnp.dot(high, low_table, preferred_element_type=jnp.float32)
        total += jnp.dot(low, high_table, preferred_element_type=jnp.float32)
        total += jnp.dot(high, high_table, preferred_element_type=jnp.float32)
        target[start : start + step, :] = total


def pack_kernel(value_hbm, key_hbm, query_hbm, cot_hbm, filter_hbm, out_ref, value_ref, key_ref, query_ref, cot_ref, filter_ref, sems):
    copies = [
        pltpu.make_async_copy(value_hbm, value_ref, sems.at[0]),
        pltpu.make_async_copy(key_hbm, key_ref, sems.at[1]),
        pltpu.make_async_copy(cot_hbm, cot_ref, sems.at[2]),
        pltpu.make_async_copy(query_hbm, query_ref, sems.at[3]),
        pltpu.make_async_copy(filter_hbm, filter_ref, sems.at[4]),
    ]
    for copy in copies:
        copy.start()
    y = lax.axis_index("y")
    tap_half, tap_channel = y // 2, y % 2
    tap_lanes = pl.ds(pl.multiple_of(tap_half * 128, 128), 128)
    tap_rows = pl.ds(pl.multiple_of(tap_channel * 64, 64), 64)
    places = [(half * 4 + j, pl.ds(j * 64, 64), pl.ds(half * 128, 128)) for j in range(2) for half in range(2)]
    copies[0].wait()
    copies[1].wait()
    for at, rows, lanes in places:
        out_ref[pl.ds(at, 64, stride=9), :] = key_ref[rows, lanes] * value_ref[rows, lanes]
    copies[2].wait()
    copies[3].wait()
    for at, rows, lanes in places:
        out_ref[pl.ds(at + 2, 64, stride=9), :] = cot_ref[rows, lanes] * query_ref[rows, lanes]
    copies[4].wait()
    out_ref[pl.ds(8, 64, stride=9), :] = filter_ref[tap_rows, tap_lanes] * (1.0 / 64)


def spectrum_rows(blocks, scratch, base, stride, sign, twiddle_ref, rowfix_ref):
    for index, value in enumerate(blocks_forward(blocks)):
        fix = (rowfix_ref[index, 0], rowfix_ref[index, 1])
        if value[1] is None:
            value = (value[0] * fix[0], value[0] * fix[1])
        else:
            value = times(value, fix)
        value = butterfly(value, sign)
        value = times(value, (twiddle_ref[index, 0], twiddle_ref[index, 1]))
        at = base + index * stride
        scratch[at : at + 8, 0:128] = value[0]
        scratch[at : at + 8, 128:256] = value[1]


def blocks_of(scratch, base, stride, sign, twiddle_ref, rowfix_ref):
    spectrum = []
    for index in range(BLOCKS):
        at = base + index * stride
        value = (scratch[at : at + 8, 0:128], scratch[at : at + 8, 128:256])
        value = times(value, (twiddle_ref[index, 0], twiddle_ref[index, 1]), True)
        value = butterfly(value, sign)
        spectrum.append(times(value, (rowfix_ref[index, 0], rowfix_ref[index, 1]), True))
    return blocks_inverse(spectrum)


def forward_kernel(signal_ref, forward_ref, inverse_ref, twiddle_ref, rowfix_ref, spec_ref, part_ref, raw, spec, taps):
    sign = half_sign()
    for y in range(4):
        at = (y // 2) * 4 + y % 2
        for c in range(0, 16, 8):
            rows = signal_ref[pl.ds((y * 16 + c) * 9 + 8, 8, stride=9), :]
            taps[pl.ds(c * 8 + at, 8, stride=8), :] = rows
            taps[pl.ds(c * 8 + at + 2, 8, stride=8), :] = rows
    spectrum_rows([taps[c * 8 : c * 8 + 8, :] for c in range(16)], raw, 544, 8, sign, twiddle_ref, rowfix_ref)
    for y in range(4):
        blocks = [signal_ref[(y * 16 + c) * 9 : (y * 16 + c) * 9 + 8, :] for c in range(16)]
        spectrum_rows(blocks, raw, y * 8, 32, sign, twiddle_ref, rowfix_ref)
    multiply(raw, spec, forward_ref, 680, 136)
    rows = lax.broadcasted_iota(jnp.int32, (8, 128), 0)
    flip = jnp.where(rows % 4 < 2, 1.0, -1.0).astype(jnp.float32)
    for index in range(BLOCKS):
        at = 544 + index * 8
        tap = (spec[at : at + 8, 0:128], spec[at : at + 8, 128:256] * flip)
        total = None
        for y in range(4):
            at = index * 32 + y * 8
            value = (spec[at : at + 8, 0:128], spec[at : at + 8, 128:256])
            product = times(value, tap)
            spec_ref[at : at + 8, 0:128] = product[0]
            spec_ref[at : at + 8, 128:256] = product[1]
            weight = (pltpu.roll(value[0], 6, 0), pltpu.roll(value[1], 6, 0))
            term = times(weight, value, True)
            total = term if total is None else add(total, term)
        raw[index * 8 : index * 8 + 8, 0:128] = total[0]
        raw[index * 8 : index * 8 + 8, 128:256] = total[1]
    multiply(raw, spec, inverse_ref, 136, 136)
    blocks = blocks_of(spec, 0, 8, sign, twiddle_ref, rowfix_ref)
    for c in range(16):
        for half in range(2):
            rows2 = blocks[c][half * 4 : half * 4 + 2, :]
            for copy in range(4):
                at = copy * 64 + c * 4 + half * 2
                part_ref[at : at + 2, :] = rows2


def inverse_kernel(spec_ref, inverse_ref, twiddle_ref, rowfix_ref, out_ref, raw):
    sign = half_sign()
    multiply(spec_ref, raw, inverse_ref, 544, 136)
    for y in range(4):
        blocks = blocks_of(raw, y * 8, 32, sign, twiddle_ref, rowfix_ref)
        for c in range(16):
            at = (y * 16 + c) * 12
            out_ref[at : at + 8, :] = blocks[c]


def filter_kernel(part_ref, message_ref, out_ref):
    out_ref[...] = message_ref[...]
    for c in range(0, 16, 2):
        pair = part_ref[c * 4 : c * 4 + 8, :]
        for copy in range(1, 4):
            pair = pair + part_ref[copy * 64 + c * 4 : copy * 64 + c * 4 + 8, :]
        pair = pair * (1.0 / 64)
        for y in range(4):
            at = (y * 16 + c) * 12
            out_ref[at + 8 : at + 12, :] = pair[0:4, :]
            out_ref[at + 20 : at + 24, :] = pair[4:8, :]


def unpack_kernel(signal_ref, value_ref, key_ref, cot_ref, query_out, key_out, value_out, filter_out):
    for j in range(2):
        rows = pl.ds(j * 64, 64)
        for half in range(2):
            lanes = pl.ds(half * 128, 128)
            at = half * 4 + j
            conv = signal_ref[pl.ds(at, 64, stride=12), :]
            grad = signal_ref[pl.ds(at + 2, 64, stride=12), :]
            query_out[rows, lanes] = cot_ref[rows, lanes] * conv
            key_out[rows, lanes] = grad * value_ref[rows, lanes]
            value_out[rows, lanes] = grad * key_ref[rows, lanes]
            filter_out[rows, lanes] = signal_ref[pl.ds(8 + half * 2 + j, 64, stride=12), :]


def call(kernel, shapes, inputs, scratch=(), copies=0, **extra):
    return pl.pallas_call(
        kernel,
        out_shape=[jax.ShapeDtypeStruct(shape, jnp.float32) for shape in shapes],
        in_specs=[HBM if copies else VMEM] * inputs,
        out_specs=[VMEM] * len(shapes),
        scratch_shapes=[pltpu.VMEM(shape, jnp.float32) for shape in scratch]
        + ([pltpu.SemaphoreType.DMA((copies,))] if copies else []),
        compiler_params=PARAMS,
        **extra,
    )


def exchange(array, axes):
    return lax.all_to_all(array, axes, split_axis=0, concat_axis=0, tiled=True)


def on_device(value_in, key_in, query_in, cotangent, filter_param):
    value_in, key_in, query_in, cotangent = value_in[0], key_in[0], query_in[0], cotangent[0]
    forward, inverse, twiddle, rowfix = [jnp.asarray(table) for table in tables()]
    pinned = [pltpu.with_memory_space_constraint(a, pltpu.HBM) for a in (value_in, key_in, query_in, cotangent, filter_param)]
    (message,) = call(pack_kernel, [(576, 128)], 5, [(128, 256)] * 5, copies=5)(
        *pinned
    )
    signal = exchange(message.reshape(64, 1, 1152), FAR).reshape(576, 128)
    spec, part = call(forward_kernel, [(544, 256), (256, 128)], 5, [(680, 256), (680, 256), (128, 128)])(
        signal, forward, inverse, twiddle, rowfix
    )
    (message,) = call(inverse_kernel, [(768, 128)], 4, [(544, 256)])(spec, inverse, twiddle, rowfix)
    part, message = lax.optimization_barrier((part, message))
    parts = exchange(part.reshape(4, 64, 128), ("zh",)).reshape(256, 128)
    (message,) = call(filter_kernel, [(768, 128)], 2)(parts, message)
    signal = exchange(message.reshape(64, 1, 1536), FAR).reshape(768, 128)
    shape = (128, 256)
    query_grad, key_grad, value_grad, filter_grad = call(unpack_kernel, [shape] * 4, 4)(
        signal, value_in, key_in, cotangent
    )
    return query_grad[None], key_grad[None], value_grad[None], filter_grad


def solution(mesh):
    fine = Mesh(mesh.devices.reshape(4, 4, 4, 2, 2), AXES)
    signal = P(("zh", "y"), None, ("x", "zl", "core"))
    taps = P(None, ("x", "zl", "core"))
    return jax.shard_map(
        on_device,
        mesh=fine,
        in_specs=(signal, signal, signal, signal, taps),
        out_specs=(signal, signal, signal, taps),
        check_vma=False,
    )
```

```python
import math

import jax
import jax.numpy as jnp
import numpy as np
from jax import lax
from jax.experimental import pallas as pl
from jax.experimental.pallas import tpu as pltpu
from jax.sharding import Mesh, PartitionSpec as P

AXES = ("zh", "y", "x", "zl", "core")
STEPS = [[(0, 1), (1, 0), (2, 3), (3, 2)], [(0, 3), (3, 0), (1, 2), (2, 1)]]
FAR = ("y", "x", "zl", "core")
BLOCKS = 17
CLASSES = [0, 16, 8, 4, 20] + [8 * j + 2 for j in range(4)] + [4 * j + 1 for j in range(8)]
VMEM = pl.BlockSpec(memory_space=pltpu.VMEM)
HBM = pl.BlockSpec(memory_space=pltpu.HBM)
PARAMS = pltpu.CompilerParams(vmem_limit_bytes=48 * 1024 * 1024)


def tables():
    lane = np.arange(128)
    forward = np.zeros((256, 256))
    angle = 2 * np.pi * np.outer(lane, lane) / 128
    c, s = np.cos(angle), np.sin(angle)
    forward = np.block([[c, -s], [s, c]])
    inverse = np.block([[c, s], [-s, c]]) * (2.0 / 8192)

    def split(table):
        high = table.astype(np.float32).astype(jnp.bfloat16)
        low = (table - high.astype(np.float64)).astype(np.float32).astype(jnp.bfloat16)
        return np.concatenate([high, low], 0)

    row_half = np.arange(8) // 4
    twiddle = np.zeros((BLOCKS, 2, 8, 128), np.float32)
    rowfix = np.zeros((BLOCKS, 2, 8, 128), np.float32)
    for index, k in enumerate(CLASSES):
        angle = -2 * np.pi * np.outer(k + 32 * row_half, lane) / 8192
        twiddle[index, 0], twiddle[index, 1] = np.cos(angle), np.sin(angle)
        angle = np.repeat((-2 * np.pi * k * row_half / 64)[:, None], 128, 1)
        rowfix[index, 0], rowfix[index, 1] = np.cos(angle), np.sin(angle)
    return split(forward), split(inverse), twiddle, rowfix


def add(a, b):
    return (a[0] + b[0], a[1] + b[1])


def sub(a, b):
    return (a[0] - b[0], a[1] - b[1])


def turn(a, step, period, sign):
    step = step % period
    if step == 0:
        return a
    if 4 * step == period:
        return (-a[1], a[0]) if sign > 0 else (a[1], -a[0])
    if 8 * step == period:
        r = np.float32(math.sqrt(0.5))
        if sign > 0:
            return ((a[0] - a[1]) * r, (a[0] + a[1]) * r)
        return ((a[0] + a[1]) * r, (a[1] - a[0]) * r)
    angle = sign * 2 * math.pi * step / period
    c, s = np.float32(math.cos(angle)), np.float32(math.sin(angle))
    return (a[0] * c - a[1] * s, a[0] * s + a[1] * c)


def small_dft(z, sign):
    n = len(z)
    if n == 1:
        return z
    even, odd = small_dft(z[0::2], sign), small_dft(z[1::2], sign)
    odd = [turn(value, j, n, sign) for j, value in enumerate(odd)]
    return [add(a, b) for a, b in zip(even, odd)] + [sub(a, b) for a, b in zip(even, odd)]


def blocks_forward(x):
    v = [x[c] + x[c + 8] for c in range(8)]
    u = [x[c] - x[c + 8] for c in range(8)]
    odd = small_dft([turn((x[c], -x[c + 8]), c, 32, -1) for c in range(8)], -1)
    two = small_dft([turn((u[c], -u[c + 4]), c, 16, -1) for c in range(4)], -1)
    a = [v[c] + v[c + 4] for c in range(4)]
    b = [v[c] - v[c + 4] for c in range(4)]
    four = small_dft([turn((b[c], -b[c + 2]), c, 8, -1) for c in range(2)], -1)
    e, o = a[0] + a[2], a[1] + a[3]
    eight = (a[0] - a[2], a[3] - a[1])
    return [(e + o, None), (e - o, None), eight] + four + two + odd


def blocks_inverse(spectrum):
    zero, sixteen, eight = spectrum[0], spectrum[1], spectrum[2]
    four, two, odd = spectrum[3:5], spectrum[5:9], spectrum[9:17]
    e, o = (zero[0] + sixteen[0]) * 0.5, (zero[0] - sixteen[0]) * 0.5
    a = [e + eight[0], o - eight[1], e - eight[0], o + eight[1]]
    g = [turn(value, c, 8, 1) for c, value in enumerate(small_dft(four, 1))]
    b = [g[0][0], g[1][0], -g[0][1], -g[1][1]]
    v = [a[c] + b[c] for c in range(4)] + [a[c] - b[c] for c in range(4)]
    g = [turn(value, c, 16, 1) for c, value in enumerate(small_dft(two, 1))]
    u = [value[0] for value in g] + [-value[1] for value in g]
    g = [turn(value, c, 32, 1) for c, value in enumerate(small_dft(odd, 1))]
    p = [v[c] + u[c] for c in range(8)]
    m = [v[c] - u[c] for c in range(8)]
    return [p[c] + g[c][0] for c in range(8)] + [m[c] - g[c][1] for c in range(8)]


def half_sign():
    rows = lax.broadcasted_iota(jnp.int32, (8, 128), 0)
    return jnp.where(rows < 4, 1.0, -1.0).astype(jnp.float32)


def swap_halves(a):
    return pltpu.roll(a, 4, 0)


def times(a, b, conjugate=False):
    if conjugate:
        return (a[0] * b[0] + a[1] * b[1], a[1] * b[0] - a[0] * b[1])
    return (a[0] * b[0] - a[1] * b[1], a[0] * b[1] + a[1] * b[0])


def butterfly(a, sign):
    return (a[0] * sign + swap_halves(a[0]), a[1] * sign + swap_halves(a[1]))


def multiply(source, target, table, rows, step):
    high_table, low_table = table[0:256, :], table[256:512, :]
    for start in range(0, rows, step):
        block = source[start : start + step, :]
        high = block.astype(jnp.bfloat16)
        low = (block - high.astype(jnp.float32)).astype(jnp.bfloat16)
        total = jnp.dot(high, low_table, preferred_element_type=jnp.float32)
        total += jnp.dot(low, high_table, preferred_element_type=jnp.float32)
        total += jnp.dot(high, high_table, preferred_element_type=jnp.float32)
        target[start : start + step, :] = total


def pack_kernel(value_hbm, key_hbm, query_hbm, cot_hbm, filter_hbm, out_ref, value_ref, key_ref, query_ref, cot_ref, filter_ref, sems):
    copies = [
        pltpu.make_async_copy(value_hbm, value_ref, sems.at[0]),
        pltpu.make_async_copy(key_hbm, key_ref, sems.at[1]),
        pltpu.make_async_copy(cot_hbm, cot_ref, sems.at[2]),
        pltpu.make_async_copy(query_hbm, query_ref, sems.at[3]),
        pltpu.make_async_copy(filter_hbm, filter_ref, sems.at[4]),
    ]
    for copy in copies:
        copy.start()
    y = lax.axis_index("y")
    tap_half, tap_channel = y // 2, y % 2
    tap_lanes = pl.ds(pl.multiple_of(tap_half * 128, 128), 128)
    tap_rows = pl.ds(pl.multiple_of(tap_channel * 64, 64), 64)
    places = [(half * 4 + j, pl.ds(j * 64, 64), pl.ds(half * 128, 128)) for j in range(2) for half in range(2)]
    copies[0].wait()
    copies[1].wait()
    for at, rows, lanes in places:
        out_ref[pl.ds(at, 64, stride=9), :] = key_ref[rows, lanes] * value_ref[rows, lanes]
    copies[2].wait()
    copies[3].wait()
    for at, rows, lanes in places:
        out_ref[pl.ds(at + 2, 64, stride=9), :] = cot_ref[rows, lanes] * query_ref[rows, lanes]
    copies[4].wait()
    out_ref[pl.ds(8, 64, stride=9), :] = filter_ref[tap_rows, tap_lanes] * (1.0 / 64)


def spectrum_rows(blocks, scratch, base, stride, sign, twiddle_ref, rowfix_ref):
    for index, value in enumerate(blocks_forward(blocks)):
        fix = (rowfix_ref[index, 0], rowfix_ref[index, 1])
        if value[1] is None:
            value = (value[0] * fix[0], value[0] * fix[1])
        else:
            value = times(value, fix)
        value = butterfly(value, sign)
        value = times(value, (twiddle_ref[index, 0], twiddle_ref[index, 1]))
        at = base + index * stride
        scratch[at : at + 8, 0:128] = value[0]
        scratch[at : at + 8, 128:256] = value[1]


def blocks_of(scratch, base, stride, sign, twiddle_ref, rowfix_ref):
    spectrum = []
    for index in range(BLOCKS):
        at = base + index * stride
        value = (scratch[at : at + 8, 0:128], scratch[at : at + 8, 128:256])
        value = times(value, (twiddle_ref[index, 0], twiddle_ref[index, 1]), True)
        value = butterfly(value, sign)
        spectrum.append(times(value, (rowfix_ref[index, 0], rowfix_ref[index, 1]), True))
    return blocks_inverse(spectrum)


def forward_kernel(signal_ref, forward_ref, inverse_ref, twiddle_ref, rowfix_ref, spec_ref, part_ref, raw, spec, taps):
    sign = half_sign()
    for y in range(4):
        at = (y // 2) * 4 + y % 2
        for c in range(0, 16, 8):
            rows = signal_ref[pl.ds((y * 16 + c) * 9 + 8, 8, stride=9), :]
            taps[pl.ds(c * 8 + at, 8, stride=8), :] = rows
            taps[pl.ds(c * 8 + at + 2, 8, stride=8), :] = rows
    spectrum_rows([taps[c * 8 : c * 8 + 8, :] for c in range(16)], raw, 544, 8, sign, twiddle_ref, rowfix_ref)
    for y in range(4):
        blocks = [signal_ref[(y * 16 + c) * 9 : (y * 16 + c) * 9 + 8, :] for c in range(16)]
        spectrum_rows(blocks, raw, y * 8, 32, sign, twiddle_ref, rowfix_ref)
    multiply(raw, spec, forward_ref, 680, 136)
    rows = lax.broadcasted_iota(jnp.int32, (8, 128), 0)
    flip = jnp.where(rows % 4 < 2, 1.0, -1.0).astype(jnp.float32)
    for index in range(BLOCKS):
        at = 544 + index * 8
        tap = (spec[at : at + 8, 0:128], spec[at : at + 8, 128:256] * flip)
        total = None
        for y in range(4):
            at = index * 32 + y * 8
            value = (spec[at : at + 8, 0:128], spec[at : at + 8, 128:256])
            product = times(value, tap)
            spec_ref[at : at + 8, 0:128] = product[0]
            spec_ref[at : at + 8, 128:256] = product[1]
            weight = (pltpu.roll(value[0], 6, 0), pltpu.roll(value[1], 6, 0))
            term = times(weight, value, True)
            total = term if total is None else add(total, term)
        raw[index * 8 : index * 8 + 8, 0:128] = total[0]
        raw[index * 8 : index * 8 + 8, 128:256] = total[1]
    multiply(raw, spec, inverse_ref, 136, 136)
    blocks = blocks_of(spec, 0, 8, sign, twiddle_ref, rowfix_ref)
    for c in range(16):
        for half in range(2):
            rows2 = blocks[c][half * 4 : half * 4 + 2, :]
            at = c * 4 + half * 2
            part_ref[at : at + 2, :] = rows2


def inverse_kernel(spec_ref, inverse_ref, twiddle_ref, rowfix_ref, out_ref, raw):
    sign = half_sign()
    multiply(spec_ref, raw, inverse_ref, 544, 136)
    for y in range(4):
        blocks = blocks_of(raw, y * 8, 32, sign, twiddle_ref, rowfix_ref)
        for c in range(16):
            at = (y * 16 + c) * 12
            out_ref[at : at + 8, :] = blocks[c]


def filter_kernel(part_ref, *refs):
    *more_refs, message_ref, out_ref = refs
    out_ref[...] = message_ref[...]
    for c in range(0, 16, 2):
        pair = part_ref[c * 4 : c * 4 + 8, :]
        for more in more_refs:
            pair = pair + more[c * 4 : c * 4 + 8, :]
        pair = pair * (1.0 / 64)
        for y in range(4):
            at = (y * 16 + c) * 12
            out_ref[at + 8 : at + 12, :] = pair[0:4, :]
            out_ref[at + 20 : at + 24, :] = pair[4:8, :]


def unpack_kernel(signal_ref, value_ref, key_ref, cot_ref, query_out, key_out, value_out, filter_out):
    for j in range(2):
        rows = pl.ds(j * 64, 64)
        for half in range(2):
            lanes = pl.ds(half * 128, 128)
            at = half * 4 + j
            conv = signal_ref[pl.ds(at, 64, stride=12), :]
            grad = signal_ref[pl.ds(at + 2, 64, stride=12), :]
            query_out[rows, lanes] = cot_ref[rows, lanes] * conv
            key_out[rows, lanes] = grad * value_ref[rows, lanes]
            value_out[rows, lanes] = grad * key_ref[rows, lanes]
            filter_out[rows, lanes] = signal_ref[pl.ds(8 + half * 2 + j, 64, stride=12), :]


def call(kernel, shapes, inputs, scratch=(), copies=0, **extra):
    return pl.pallas_call(
        kernel,
        out_shape=[jax.ShapeDtypeStruct(shape, jnp.float32) for shape in shapes],
        in_specs=[HBM if copies else VMEM] * inputs,
        out_specs=[VMEM] * len(shapes),
        scratch_shapes=[pltpu.VMEM(shape, jnp.float32) for shape in scratch]
        + ([pltpu.SemaphoreType.DMA((copies,))] if copies else []),
        compiler_params=PARAMS,
        **extra,
    )


def exchange(array, axes):
    return lax.all_to_all(array, axes, split_axis=0, concat_axis=0, tiled=True)


def on_device(value_in, key_in, query_in, cotangent, filter_param):
    value_in, key_in, query_in, cotangent = value_in[0], key_in[0], query_in[0], cotangent[0]
    forward, inverse, twiddle, rowfix = [jnp.asarray(table) for table in tables()]
    pinned = [pltpu.with_memory_space_constraint(a, pltpu.HBM) for a in (value_in, key_in, query_in, cotangent, filter_param)]
    (message,) = call(pack_kernel, [(576, 128)], 5, [(128, 256)] * 5, copies=5)(
        *pinned
    )
    signal = exchange(message.reshape(64, 1, 1152), FAR).reshape(576, 128)
    spec, part = call(forward_kernel, [(544, 256), (64, 128)], 5, [(680, 256), (680, 256), (128, 128)])(
        signal, forward, inverse, twiddle, rowfix
    )
    (message,) = call(inverse_kernel, [(768, 128)], 4, [(544, 256)])(spec, inverse, twiddle, rowfix)
    for pairs in STEPS:
        part = part + lax.ppermute(part, "zh", pairs)
    parts = [part]
    (message,) = call(filter_kernel, [(768, 128)], 2)(*parts, message)
    signal = exchange(message.reshape(64, 1, 1536), FAR).reshape(768, 128)
    shape = (128, 256)
    query_grad, key_grad, value_grad, filter_grad = call(unpack_kernel, [shape] * 4, 4)(
        signal, value_in, key_in, cotangent
    )
    return query_grad[None], key_grad[None], value_grad[None], filter_grad


def solution(mesh):
    fine = Mesh(mesh.devices.reshape(4, 4, 4, 2, 2), AXES)
    signal = P(("zh", "y"), None, ("x", "zl", "core"))
    taps = P(None, ("x", "zl", "core"))
    return jax.shard_map(
        on_device,
        mesh=fine,
        in_specs=(signal, signal, signal, signal, taps),
        out_specs=(signal, signal, signal, taps),
        check_vma=False,
    )
```

```python
import math

import jax
import jax.numpy as jnp
import numpy as np
from jax import lax
from jax.experimental import pallas as pl
from jax.experimental.pallas import tpu as pltpu
from jax.sharding import Mesh, PartitionSpec as P

AXES = ("zh", "y", "x", "zl", "core")
STEPS = [
    [(2 * zh + core, 2 * other + 1 - core) for zh, other in enumerate(order) for core in range(2)]
    for order in ((3, 2, 1, 0), (1, 0, 3, 2))
]
FAR = ("y", "x", "zl", "core")
BLOCKS = 17
CLASSES = [0, 16, 8, 4, 20] + [8 * j + 2 for j in range(4)] + [4 * j + 1 for j in range(8)]
VMEM = pl.BlockSpec(memory_space=pltpu.VMEM)
HBM = pl.BlockSpec(memory_space=pltpu.HBM)
PARAMS = pltpu.CompilerParams(vmem_limit_bytes=48 * 1024 * 1024)


def tables():
    lane = np.arange(128)
    forward = np.zeros((256, 256))
    angle = 2 * np.pi * np.outer(lane, lane) / 128
    c, s = np.cos(angle), np.sin(angle)
    forward = np.block([[c, -s], [s, c]])
    inverse = np.block([[c, s], [-s, c]]) * (2.0 / 8192)

    def split(table):
        high = table.astype(np.float32).astype(jnp.bfloat16)
        low = (table - high.astype(np.float64)).astype(np.float32).astype(jnp.bfloat16)
        return np.concatenate([high, low], 0)

    row_half = np.arange(8) // 4
    twiddle = np.zeros((BLOCKS, 2, 8, 128), np.float32)
    rowfix = np.zeros((BLOCKS, 2, 8, 128), np.float32)
    for index, k in enumerate(CLASSES):
        angle = -2 * np.pi * np.outer(k + 32 * row_half, lane) / 8192
        twiddle[index, 0], twiddle[index, 1] = np.cos(angle), np.sin(angle)
        angle = np.repeat((-2 * np.pi * k * row_half / 64)[:, None], 128, 1)
        rowfix[index, 0], rowfix[index, 1] = np.cos(angle), np.sin(angle)
    return split(forward), split(inverse), twiddle, rowfix


def add(a, b):
    return (a[0] + b[0], a[1] + b[1])


def sub(a, b):
    return (a[0] - b[0], a[1] - b[1])


def turn(a, step, period, sign):
    step = step % period
    if step == 0:
        return a
    if 4 * step == period:
        return (-a[1], a[0]) if sign > 0 else (a[1], -a[0])
    if 8 * step == period:
        r = np.float32(math.sqrt(0.5))
        if sign > 0:
            return ((a[0] - a[1]) * r, (a[0] + a[1]) * r)
        return ((a[0] + a[1]) * r, (a[1] - a[0]) * r)
    angle = sign * 2 * math.pi * step / period
    c, s = np.float32(math.cos(angle)), np.float32(math.sin(angle))
    return (a[0] * c - a[1] * s, a[0] * s + a[1] * c)


def small_dft(z, sign):
    n = len(z)
    if n == 1:
        return z
    even, odd = small_dft(z[0::2], sign), small_dft(z[1::2], sign)
    odd = [turn(value, j, n, sign) for j, value in enumerate(odd)]
    return [add(a, b) for a, b in zip(even, odd)] + [sub(a, b) for a, b in zip(even, odd)]


def blocks_forward(x):
    v = [x[c] + x[c + 8] for c in range(8)]
    u = [x[c] - x[c + 8] for c in range(8)]
    odd = small_dft([turn((x[c], -x[c + 8]), c, 32, -1) for c in range(8)], -1)
    two = small_dft([turn((u[c], -u[c + 4]), c, 16, -1) for c in range(4)], -1)
    a = [v[c] + v[c + 4] for c in range(4)]
    b = [v[c] - v[c + 4] for c in range(4)]
    four = small_dft([turn((b[c], -b[c + 2]), c, 8, -1) for c in range(2)], -1)
    e, o = a[0] + a[2], a[1] + a[3]
    eight = (a[0] - a[2], a[3] - a[1])
    return [(e + o, None), (e - o, None), eight] + four + two + odd


def blocks_inverse(spectrum):
    zero, sixteen, eight = spectrum[0], spectrum[1], spectrum[2]
    four, two, odd = spectrum[3:5], spectrum[5:9], spectrum[9:17]
    e, o = (zero[0] + sixteen[0]) * 0.5, (zero[0] - sixteen[0]) * 0.5
    a = [e + eight[0], o - eight[1], e - eight[0], o + eight[1]]
    g = [turn(value, c, 8, 1) for c, value in enumerate(small_dft(four, 1))]
    b = [g[0][0], g[1][0], -g[0][1], -g[1][1]]
    v = [a[c] + b[c] for c in range(4)] + [a[c] - b[c] for c in range(4)]
    g = [turn(value, c, 16, 1) for c, value in enumerate(small_dft(two, 1))]
    u = [value[0] for value in g] + [-value[1] for value in g]
    g = [turn(value, c, 32, 1) for c, value in enumerate(small_dft(odd, 1))]
    p = [v[c] + u[c] for c in range(8)]
    m = [v[c] - u[c] for c in range(8)]
    return [p[c] + g[c][0] for c in range(8)] + [m[c] - g[c][1] for c in range(8)]


def half_sign():
    rows = lax.broadcasted_iota(jnp.int32, (8, 128), 0)
    return jnp.where(rows < 4, 1.0, -1.0).astype(jnp.float32)


def swap_halves(a):
    return pltpu.roll(a, 4, 0)


def times(a, b, conjugate=False):
    if conjugate:
        return (a[0] * b[0] + a[1] * b[1], a[1] * b[0] - a[0] * b[1])
    return (a[0] * b[0] - a[1] * b[1], a[0] * b[1] + a[1] * b[0])


def butterfly(a, sign):
    return (a[0] * sign + swap_halves(a[0]), a[1] * sign + swap_halves(a[1]))


def multiply(source, target, table, rows, step):
    high_table, low_table = table[0:256, :], table[256:512, :]
    for start in range(0, rows, step):
        block = source[start : start + step, :]
        high = block.astype(jnp.bfloat16)
        low = (block - high.astype(jnp.float32)).astype(jnp.bfloat16)
        total = jnp.dot(high, low_table, preferred_element_type=jnp.float32)
        total += jnp.dot(low, high_table, preferred_element_type=jnp.float32)
        total += jnp.dot(high, high_table, preferred_element_type=jnp.float32)
        target[start : start + step, :] = total


def channel_bases():
    odd = lax.axis_index("zh") % 2
    return odd * 64, (1 - odd) * 64


def pack_kernel(value_hbm, key_hbm, query_hbm, cot_hbm, filter_hbm, out_ref, value_ref, key_ref, query_ref, cot_ref, filter_ref, sems):
    copies = [
        pltpu.make_async_copy(value_hbm, value_ref, sems.at[0]),
        pltpu.make_async_copy(key_hbm, key_ref, sems.at[1]),
        pltpu.make_async_copy(cot_hbm, cot_ref, sems.at[2]),
        pltpu.make_async_copy(query_hbm, query_ref, sems.at[3]),
        pltpu.make_async_copy(filter_hbm, filter_ref, sems.at[4]),
    ]
    for copy in copies:
        copy.start()
    y, bases = lax.axis_index("y"), channel_bases()
    tap_half, tap_channel = y // 2, y % 2
    tap_lanes = pl.ds(pl.multiple_of(tap_half * 128, 128), 128)
    places = [
        (core * 9 + half * 4 + j, pl.ds(pl.multiple_of(bases[core] + j * 32, 32), 32), pl.ds(half * 128, 128))
        for core in range(2)
        for j in range(2)
        for half in range(2)
    ]
    copies[0].wait()
    copies[1].wait()
    for at, rows, lanes in places:
        out_ref[pl.ds(at, 32, stride=18), :] = key_ref[rows, lanes] * value_ref[rows, lanes]
    copies[2].wait()
    copies[3].wait()
    for at, rows, lanes in places:
        out_ref[pl.ds(at + 2, 32, stride=18), :] = cot_ref[rows, lanes] * query_ref[rows, lanes]
    copies[4].wait()
    for core in range(2):
        rows = pl.ds(pl.multiple_of(bases[core] + tap_channel * 32, 32), 32)
        out_ref[pl.ds(core * 9 + 8, 32, stride=18), :] = filter_ref[rows, tap_lanes] * (1.0 / 64)


def spectrum_rows(blocks, scratch, base, stride, sign, twiddle_ref, rowfix_ref):
    for index, value in enumerate(blocks_forward(blocks)):
        fix = (rowfix_ref[index, 0], rowfix_ref[index, 1])
        if value[1] is None:
            value = (value[0] * fix[0], value[0] * fix[1])
        else:
            value = times(value, fix)
        value = butterfly(value, sign)
        value = times(value, (twiddle_ref[index, 0], twiddle_ref[index, 1]))
        at = base + index * stride
        scratch[at : at + 8, 0:128] = value[0]
        scratch[at : at + 8, 128:256] = value[1]


def blocks_of(scratch, base, stride, sign, twiddle_ref, rowfix_ref):
    spectrum = []
    for index in range(BLOCKS):
        at = base + index * stride
        value = (scratch[at : at + 8, 0:128], scratch[at : at + 8, 128:256])
        value = times(value, (twiddle_ref[index, 0], twiddle_ref[index, 1]), True)
        value = butterfly(value, sign)
        spectrum.append(times(value, (rowfix_ref[index, 0], rowfix_ref[index, 1]), True))
    return blocks_inverse(spectrum)


def forward_kernel(signal_ref, forward_ref, inverse_ref, twiddle_ref, rowfix_ref, spec_ref, part_ref, raw, spec, taps):
    sign = half_sign()
    for y in range(4):
        at = (y // 2) * 4 + y % 2
        for c in range(0, 16, 8):
            rows = signal_ref[pl.ds((y * 16 + c) * 9 + 8, 8, stride=9), :]
            taps[pl.ds(c * 8 + at, 8, stride=8), :] = rows
            taps[pl.ds(c * 8 + at + 2, 8, stride=8), :] = rows
    spectrum_rows([taps[c * 8 : c * 8 + 8, :] for c in range(16)], raw, 544, 8, sign, twiddle_ref, rowfix_ref)
    for y in range(4):
        blocks = [signal_ref[(y * 16 + c) * 9 : (y * 16 + c) * 9 + 8, :] for c in range(16)]
        spectrum_rows(blocks, raw, y * 8, 32, sign, twiddle_ref, rowfix_ref)
    multiply(raw, spec, forward_ref, 680, 136)
    rows = lax.broadcasted_iota(jnp.int32, (8, 128), 0)
    flip = jnp.where(rows % 4 < 2, 1.0, -1.0).astype(jnp.float32)
    for index in range(BLOCKS):
        at = 544 + index * 8
        tap = (spec[at : at + 8, 0:128], spec[at : at + 8, 128:256] * flip)
        total = None
        for y in range(4):
            at = index * 32 + y * 8
            value = (spec[at : at + 8, 0:128], spec[at : at + 8, 128:256])
            product = times(value, tap)
            spec_ref[at : at + 8, 0:128] = product[0]
            spec_ref[at : at + 8, 128:256] = product[1]
            weight = (pltpu.roll(value[0], 6, 0), pltpu.roll(value[1], 6, 0))
            term = times(weight, value, True)
            total = term if total is None else add(total, term)
        raw[index * 8 : index * 8 + 8, 0:128] = total[0]
        raw[index * 8 : index * 8 + 8, 128:256] = total[1]
    multiply(raw, spec, inverse_ref, 136, 136)
    blocks = blocks_of(spec, 0, 8, sign, twiddle_ref, rowfix_ref)
    for c in range(16):
        for half in range(2):
            rows2 = blocks[c][half * 4 : half * 4 + 2, :]
            at = c * 4 + half * 2
            part_ref[at : at + 2, :] = rows2


def inverse_kernel(spec_ref, inverse_ref, twiddle_ref, rowfix_ref, out_ref, raw):
    sign = half_sign()
    multiply(spec_ref, raw, inverse_ref, 544, 136)
    for y in range(4):
        blocks = blocks_of(raw, y * 8, 32, sign, twiddle_ref, rowfix_ref)
        for c in range(16):
            at = (y * 16 + c) * 12
            out_ref[at : at + 8, :] = blocks[c]


def filter_kernel(part_ref, *refs):
    *more_refs, message_ref, out_ref = refs
    out_ref[...] = message_ref[...]
    for c in range(0, 16, 2):
        pair = part_ref[c * 4 : c * 4 + 8, :]
        for more in more_refs:
            pair = pair + more[c * 4 : c * 4 + 8, :]
        pair = pair * (1.0 / 64)
        for y in range(4):
            at = (y * 16 + c) * 12
            out_ref[at + 8 : at + 12, :] = pair[0:4, :]
            out_ref[at + 20 : at + 24, :] = pair[4:8, :]


def unpack_kernel(signal_ref, value_ref, key_ref, cot_ref, query_out, key_out, value_out, filter_out):
    bases = channel_bases()
    for core in range(2):
        for j in range(2):
            rows = pl.ds(pl.multiple_of(bases[core] + j * 32, 32), 32)
            for half in range(2):
                lanes = pl.ds(half * 128, 128)
                at = core * 12 + half * 4 + j
                conv = signal_ref[pl.ds(at, 32, stride=24), :]
                grad = signal_ref[pl.ds(at + 2, 32, stride=24), :]
                query_out[rows, lanes] = cot_ref[rows, lanes] * conv
                key_out[rows, lanes] = grad * value_ref[rows, lanes]
                value_out[rows, lanes] = grad * key_ref[rows, lanes]
                filter_out[rows, lanes] = signal_ref[pl.ds(core * 12 + 8 + half * 2 + j, 32, stride=24), :]


def call(kernel, shapes, inputs, scratch=(), copies=0, **extra):
    return pl.pallas_call(
        kernel,
        out_shape=[jax.ShapeDtypeStruct(shape, jnp.float32) for shape in shapes],
        in_specs=[HBM if copies else VMEM] * inputs,
        out_specs=[VMEM] * len(shapes),
        scratch_shapes=[pltpu.VMEM(shape, jnp.float32) for shape in scratch]
        + ([pltpu.SemaphoreType.DMA((copies,))] if copies else []),
        compiler_params=PARAMS,
        **extra,
    )


def exchange(array, axes):
    return lax.all_to_all(array, axes, split_axis=0, concat_axis=0, tiled=True)


def on_device(value_in, key_in, query_in, cotangent, filter_param):
    value_in, key_in, query_in, cotangent = value_in[0], key_in[0], query_in[0], cotangent[0]
    forward, inverse, twiddle, rowfix = [jnp.asarray(table) for table in tables()]
    pinned = [pltpu.with_memory_space_constraint(a, pltpu.HBM) for a in (value_in, key_in, query_in, cotangent, filter_param)]
    (message,) = call(pack_kernel, [(576, 128)], 5, [(128, 256)] * 5, copies=5)(
        *pinned
    )
    signal = exchange(message.reshape(64, 1, 1152), FAR).reshape(576, 128)
    spec, part = call(forward_kernel, [(544, 256), (64, 128)], 5, [(680, 256), (680, 256), (128, 128)])(
        signal, forward, inverse, twiddle, rowfix
    )
    (message,) = call(inverse_kernel, [(768, 128)], 4, [(544, 256)])(spec, inverse, twiddle, rowfix)
    for pairs in STEPS:
        part = part + lax.ppermute(part, ("zh", "core"), pairs)
    parts = [part]
    (message,) = call(filter_kernel, [(768, 128)], 2)(*parts, message)
    signal = exchange(message.reshape(64, 1, 1536), FAR).reshape(768, 128)
    shape = (128, 256)
    query_grad, key_grad, value_grad, filter_grad = call(unpack_kernel, [shape] * 4, 4)(
        signal, value_in, key_in, cotangent
    )
    return query_grad[None], key_grad[None], value_grad[None], filter_grad


def solution(mesh):
    fine = Mesh(mesh.devices.reshape(4, 4, 4, 2, 2), AXES)
    signal = P(("zh", "y"), None, ("x", "zl", "core"))
    taps = P(None, ("x", "zl", "core"))
    return jax.shard_map(
        on_device,
        mesh=fine,
        in_specs=(signal, signal, signal, signal, taps),
        out_specs=(signal, signal, signal, taps),
        check_vma=False,
    )
```

```python
import math

import jax
import jax.numpy as jnp
import numpy as np
from jax import lax
from jax.experimental import pallas as pl
from jax.experimental.pallas import tpu as pltpu
from jax.sharding import Mesh, PartitionSpec as P

AXES = ("zh", "y", "x", "zl", "core")
ORDERS = ((3, 2, 1, 0), (1, 0, 3, 2))
STEPS = [
    [
        (2 * zh + core, 2 * ORDERS[(step + core + zh + 0) % 2][zh] + 1 - core)
        for zh in range(4)
        for core in range(2)
    ]
    for step in range(2)
]
FAR = ("y", "x", "zl", "core")
BLOCKS = 17
CLASSES = [0, 16, 8, 4, 20] + [8 * j + 2 for j in range(4)] + [4 * j + 1 for j in range(8)]
VMEM = pl.BlockSpec(memory_space=pltpu.VMEM)
HBM = pl.BlockSpec(memory_space=pltpu.HBM)
PARAMS = pltpu.CompilerParams(vmem_limit_bytes=48 * 1024 * 1024)


def tables():
    lane = np.arange(128)
    forward = np.zeros((256, 256))
    angle = 2 * np.pi * np.outer(lane, lane) / 128
    c, s = np.cos(angle), np.sin(angle)
    forward = np.block([[c, -s], [s, c]])
    inverse = np.block([[c, s], [-s, c]]) * (2.0 / 8192)

    def split(table):
        high = table.astype(np.float32).astype(jnp.bfloat16)
        low = (table - high.astype(np.float64)).astype(np.float32).astype(jnp.bfloat16)
        return np.concatenate([high, low], 0)

    row_half = np.arange(8) // 4
    twiddle = np.zeros((BLOCKS, 2, 8, 128), np.float32)
    rowfix = np.zeros((BLOCKS, 2, 8, 128), np.float32)
    for index, k in enumerate(CLASSES):
        angle = -2 * np.pi * np.outer(k + 32 * row_half, lane) / 8192
        twiddle[index, 0], twiddle[index, 1] = np.cos(angle), np.sin(angle)
        angle = np.repeat((-2 * np.pi * k * row_half / 64)[:, None], 128, 1)
        rowfix[index, 0], rowfix[index, 1] = np.cos(angle), np.sin(angle)
    return split(forward), split(inverse), twiddle, rowfix


def add(a, b):
    return (a[0] + b[0], a[1] + b[1])


def sub(a, b):
    return (a[0] - b[0], a[1] - b[1])


def turn(a, step, period, sign):
    step = step % period
    if step == 0:
        return a
    if 4 * step == period:
        return (-a[1], a[0]) if sign > 0 else (a[1], -a[0])
    if 8 * step == period:
        r = np.float32(math.sqrt(0.5))
        if sign > 0:
            return ((a[0] - a[1]) * r, (a[0] + a[1]) * r)
        return ((a[0] + a[1]) * r, (a[1] - a[0]) * r)
    angle = sign * 2 * math.pi * step / period
    c, s = np.float32(math.cos(angle)), np.float32(math.sin(angle))
    return (a[0] * c - a[1] * s, a[0] * s + a[1] * c)


def small_dft(z, sign):
    n = len(z)
    if n == 1:
        return z
    even, odd = small_dft(z[0::2], sign), small_dft(z[1::2], sign)
    odd = [turn(value, j, n, sign) for j, value in enumerate(odd)]
    return [add(a, b) for a, b in zip(even, odd)] + [sub(a, b) for a, b in zip(even, odd)]


def blocks_forward(x):
    v = [x[c] + x[c + 8] for c in range(8)]
    u = [x[c] - x[c + 8] for c in range(8)]
    odd = small_dft([turn((x[c], -x[c + 8]), c, 32, -1) for c in range(8)], -1)
    two = small_dft([turn((u[c], -u[c + 4]), c, 16, -1) for c in range(4)], -1)
    a = [v[c] + v[c + 4] for c in range(4)]
    b = [v[c] - v[c + 4] for c in range(4)]
    four = small_dft([turn((b[c], -b[c + 2]), c, 8, -1) for c in range(2)], -1)
    e, o = a[0] + a[2], a[1] + a[3]
    eight = (a[0] - a[2], a[3] - a[1])
    return [(e + o, None), (e - o, None), eight] + four + two + odd


def blocks_inverse(spectrum):
    zero, sixteen, eight = spectrum[0], spectrum[1], spectrum[2]
    four, two, odd = spectrum[3:5], spectrum[5:9], spectrum[9:17]
    e, o = (zero[0] + sixteen[0]) * 0.5, (zero[0] - sixteen[0]) * 0.5
    a = [e + eight[0], o - eight[1], e - eight[0], o + eight[1]]
    g = [turn(value, c, 8, 1) for c, value in enumerate(small_dft(four, 1))]
    b = [g[0][0], g[1][0], -g[0][1], -g[1][1]]
    v = [a[c] + b[c] for c in range(4)] + [a[c] - b[c] for c in range(4)]
    g = [turn(value, c, 16, 1) for c, value in enumerate(small_dft(two, 1))]
    u = [value[0] for value in g] + [-value[1] for value in g]
    g = [turn(value, c, 32, 1) for c, value in enumerate(small_dft(odd, 1))]
    p = [v[c] + u[c] for c in range(8)]
    m = [v[c] - u[c] for c in range(8)]
    return [p[c] + g[c][0] for c in range(8)] + [m[c] - g[c][1] for c in range(8)]


def half_sign():
    rows = lax.broadcasted_iota(jnp.int32, (8, 128), 0)
    return jnp.where(rows < 4, 1.0, -1.0).astype(jnp.float32)


def swap_halves(a):
    return pltpu.roll(a, 4, 0)


def times(a, b, conjugate=False):
    if conjugate:
        return (a[0] * b[0] + a[1] * b[1], a[1] * b[0] - a[0] * b[1])
    return (a[0] * b[0] - a[1] * b[1], a[0] * b[1] + a[1] * b[0])


def butterfly(a, sign):
    return (a[0] * sign + swap_halves(a[0]), a[1] * sign + swap_halves(a[1]))


def multiply(source, target, table, start):
    high_table, low_table = table[0:256, :], table[256:512, :]
    block = source[start : start + 136, :]
    high = block.astype(jnp.bfloat16)
    low = (block - high.astype(jnp.float32)).astype(jnp.bfloat16)
    total = jnp.dot(high, low_table, preferred_element_type=jnp.float32)
    total += jnp.dot(low, high_table, preferred_element_type=jnp.float32)
    total += jnp.dot(high, high_table, preferred_element_type=jnp.float32)
    target[start : start + 136, :] = total


def channel_bases():
    odd = lax.axis_index("zh") % 2
    return odd * 64, (1 - odd) * 64


def pack_kernel(value_hbm, key_hbm, query_hbm, cot_hbm, filter_hbm, out_ref, value_ref, key_ref, query_ref, cot_ref, filter_ref, sems):
    copies = [
        pltpu.make_async_copy(value_hbm, value_ref, sems.at[0]),
        pltpu.make_async_copy(key_hbm, key_ref, sems.at[1]),
        pltpu.make_async_copy(cot_hbm, cot_ref, sems.at[2]),
        pltpu.make_async_copy(query_hbm, query_ref, sems.at[3]),
        pltpu.make_async_copy(filter_hbm, filter_ref, sems.at[4]),
    ]
    for copy in copies:
        copy.start()
    y, bases = lax.axis_index("y"), channel_bases()
    tap_half, tap_channel = y // 2, y % 2
    tap_lanes = pl.ds(pl.multiple_of(tap_half * 128, 128), 128)
    places = [
        (core * 9 + half * 4 + j, pl.ds(pl.multiple_of(bases[core] + j * 32, 32), 32), pl.ds(half * 128, 128))
        for core in range(2)
        for j in range(2)
        for half in range(2)
    ]
    copies[0].wait()
    copies[1].wait()
    for at, rows, lanes in places:
        out_ref[pl.ds(at, 32, stride=18), :] = key_ref[rows, lanes] * value_ref[rows, lanes]
    copies[2].wait()
    copies[3].wait()
    for at, rows, lanes in places:
        out_ref[pl.ds(at + 2, 32, stride=18), :] = cot_ref[rows, lanes] * query_ref[rows, lanes]
    copies[4].wait()
    for core in range(2):
        rows = pl.ds(pl.multiple_of(bases[core] + tap_channel * 32, 32), 32)
        out_ref[pl.ds(core * 9 + 8, 32, stride=18), :] = filter_ref[rows, tap_lanes] * (1.0 / 64)


def spectrum_rows(blocks, scratch, base, sign, twiddle_ref, rowfix_ref):
    for index, value in enumerate(blocks_forward(blocks)):
        fix = (rowfix_ref[index, 0], rowfix_ref[index, 1])
        if value[1] is None:
            value = (value[0] * fix[0], value[0] * fix[1])
        else:
            value = times(value, fix)
        value = butterfly(value, sign)
        value = times(value, (twiddle_ref[index, 0], twiddle_ref[index, 1]))
        at = base + index * 8
        scratch[at : at + 8, 0:128] = value[0]
        scratch[at : at + 8, 128:256] = value[1]


def blocks_of(scratch, base, sign, twiddle_ref, rowfix_ref):
    spectrum = []
    for index in range(BLOCKS):
        at = base + index * 8
        value = (scratch[at : at + 8, 0:128], scratch[at : at + 8, 128:256])
        value = times(value, (twiddle_ref[index, 0], twiddle_ref[index, 1]), True)
        value = butterfly(value, sign)
        spectrum.append(times(value, (rowfix_ref[index, 0], rowfix_ref[index, 1]), True))
    return blocks_inverse(spectrum)


def forward_kernel(signal_ref, forward_ref, inverse_ref, twiddle_ref, rowfix_ref, spec_ref, part_ref, raw):
    sign = half_sign()
    for y in range(4):
        blocks = [signal_ref[(y * 16 + c) * 9 : (y * 16 + c) * 9 + 8, :] for c in range(16)]
        spectrum_rows(blocks, raw, y * 136, sign, twiddle_ref, rowfix_ref)
        multiply(raw, spec_ref, forward_ref, y * 136)
    for index in range(BLOCKS):
        total = None
        for y in range(4):
            at = y * 136 + index * 8
            value = (spec_ref[at : at + 8, 0:128], spec_ref[at : at + 8, 128:256])
            weight = (pltpu.roll(value[0], 6, 0), pltpu.roll(value[1], 6, 0))
            term = times(weight, value, True)
            total = term if total is None else add(total, term)
        raw[544 + index * 8 : 552 + index * 8, 0:128] = total[0]
        raw[544 + index * 8 : 552 + index * 8, 128:256] = total[1]
    multiply(raw, raw, inverse_ref, 544)
    blocks = blocks_of(raw, 544, sign, twiddle_ref, rowfix_ref)
    for c in range(16):
        for half in range(2):
            at = c * 4 + half * 2
            part_ref[at : at + 2, :] = blocks[c][half * 4 : half * 4 + 2, :]


def inverse_kernel(signal_ref, spec_ref, forward_ref, inverse_ref, twiddle_ref, rowfix_ref, out_ref, raw, spec, taps):
    sign = half_sign()
    for y in range(4):
        at = (y // 2) * 4 + y % 2
        for c in range(0, 16, 8):
            rows = signal_ref[pl.ds((y * 16 + c) * 9 + 8, 8, stride=9), :]
            taps[pl.ds(c * 8 + at, 8, stride=8), :] = rows
            taps[pl.ds(c * 8 + at + 2, 8, stride=8), :] = rows
    spectrum_rows([taps[c * 8 : c * 8 + 8, :] for c in range(16)], raw, 544, sign, twiddle_ref, rowfix_ref)
    multiply(raw, spec, forward_ref, 544)
    rows = lax.broadcasted_iota(jnp.int32, (8, 128), 0)
    flip = jnp.where(rows % 4 < 2, 1.0, -1.0).astype(jnp.float32)
    for y in range(4):
        for index in range(BLOCKS):
            at = 544 + index * 8
            tap = (spec[at : at + 8, 0:128], spec[at : at + 8, 128:256] * flip)
            at = y * 136 + index * 8
            value = times((spec_ref[at : at + 8, 0:128], spec_ref[at : at + 8, 128:256]), tap)
            raw[at : at + 8, 0:128] = value[0]
            raw[at : at + 8, 128:256] = value[1]
        multiply(raw, spec, inverse_ref, y * 136)
        blocks = blocks_of(spec, y * 136, sign, twiddle_ref, rowfix_ref)
        for c in range(16):
            at = (y * 16 + c) * 12
            out_ref[at : at + 8, :] = blocks[c]


def filter_kernel(part_ref, *refs):
    *more_refs, message_ref, out_ref = refs
    out_ref[...] = message_ref[...]
    for c in range(0, 16, 2):
        pair = part_ref[c * 4 : c * 4 + 8, :]
        for more in more_refs:
            pair = pair + more[c * 4 : c * 4 + 8, :]
        pair = pair * (1.0 / 64)
        for y in range(4):
            at = (y * 16 + c) * 12
            out_ref[at + 8 : at + 12, :] = pair[0:4, :]
            out_ref[at + 20 : at + 24, :] = pair[4:8, :]


def unpack_kernel(signal_ref, value_ref, key_ref, cot_ref, query_out, key_out, value_out, filter_out):
    bases = channel_bases()
    for core in range(2):
        for j in range(2):
            rows = pl.ds(pl.multiple_of(bases[core] + j * 32, 32), 32)
            for half in range(2):
                lanes = pl.ds(half * 128, 128)
                at = core * 12 + half * 4 + j
                conv = signal_ref[pl.ds(at, 32, stride=24), :]
                grad = signal_ref[pl.ds(at + 2, 32, stride=24), :]
                query_out[rows, lanes] = cot_ref[rows, lanes] * conv
                key_out[rows, lanes] = grad * value_ref[rows, lanes]
                value_out[rows, lanes] = grad * key_ref[rows, lanes]
                filter_out[rows, lanes] = signal_ref[pl.ds(core * 12 + 8 + half * 2 + j, 32, stride=24), :]


def call(kernel, shapes, inputs, scratch=(), copies=0, **extra):
    return pl.pallas_call(
        kernel,
        out_shape=[jax.ShapeDtypeStruct(shape, jnp.float32) for shape in shapes],
        in_specs=[HBM if copies else VMEM] * inputs,
        out_specs=[VMEM] * len(shapes),
        scratch_shapes=[pltpu.VMEM(shape, jnp.float32) for shape in scratch]
        + ([pltpu.SemaphoreType.DMA((copies,))] if copies else []),
        compiler_params=PARAMS,
        **extra,
    )


def exchange(array, axes):
    return lax.all_to_all(array, axes, split_axis=0, concat_axis=0, tiled=True)


def on_device(value_in, key_in, query_in, cotangent, filter_param):
    value_in, key_in, query_in, cotangent = value_in[0], key_in[0], query_in[0], cotangent[0]
    forward, inverse, twiddle, rowfix = [jnp.asarray(table) for table in tables()]
    pinned = [pltpu.with_memory_space_constraint(a, pltpu.HBM) for a in (value_in, key_in, query_in, cotangent, filter_param)]
    (message,) = call(pack_kernel, [(576, 128)], 5, [(128, 256)] * 5, copies=5)(
        *pinned
    )
    signal = exchange(message.reshape(64, 1, 1152), FAR).reshape(576, 128)
    spec, part = call(forward_kernel, [(544, 256), (64, 128)], 5, [(680, 256)])(
        signal, forward, inverse, twiddle, rowfix
    )
    for pairs in STEPS:
        part = part + lax.ppermute(part, ("zh", "core"), pairs)
    (message,) = call(inverse_kernel, [(768, 128)], 6, [(680, 256)] * 2 + [(128, 128)])(
        signal, spec, forward, inverse, twiddle, rowfix
    )
    (message,) = call(filter_kernel, [(768, 128)], 2)(part, message)
    signal = exchange(message.reshape(64, 1, 1536), FAR).reshape(768, 128)
    shape = (128, 256)
    query_grad, key_grad, value_grad, filter_grad = call(unpack_kernel, [shape] * 4, 4)(
        signal, value_in, key_in, cotangent
    )
    return query_grad[None], key_grad[None], value_grad[None], filter_grad


def solution(mesh):
    fine = Mesh(mesh.devices.reshape(4, 4, 4, 2, 2), AXES)
    signal = P(("zh", "y"), None, ("x", "zl", "core"))
    taps = P(None, ("x", "zl", "core"))
    return jax.shard_map(
        on_device,
        mesh=fine,
        in_specs=(signal, signal, signal, signal, taps),
        out_specs=(signal, signal, signal, taps),
        check_vma=False,
    )
```

```python
import math

import jax
import jax.numpy as jnp
import numpy as np
from jax import lax
from jax.experimental import pallas as pl
from jax.experimental.pallas import tpu as pltpu
from jax.sharding import Mesh, PartitionSpec as P

AXES = ("zh", "y", "x", "zl", "core")
ORDERS = ((3, 2, 1, 0), (1, 0, 3, 2))
STEPS = [
    [
        (2 * zh + core, 2 * ORDERS[(step + core + zh + 0) % 2][zh] + 1 - core)
        for zh in range(4)
        for core in range(2)
    ]
    for step in range(2)
]
FAR = ("y", "x", "zl", "core")
BLOCKS = 17
CLASSES = [0, 16, 8, 4, 20] + [8 * j + 2 for j in range(4)] + [4 * j + 1 for j in range(8)]
VMEM = pl.BlockSpec(memory_space=pltpu.VMEM)
HBM = pl.BlockSpec(memory_space=pltpu.HBM)
PARAMS = pltpu.CompilerParams(vmem_limit_bytes=48 * 1024 * 1024)


def tables():
    lane = np.arange(128)
    forward = np.zeros((256, 256))
    angle = 2 * np.pi * np.outer(lane, lane) / 128
    c, s = np.cos(angle), np.sin(angle)
    forward = np.block([[c, -s], [s, c]])
    inverse = np.block([[c, s], [-s, c]]) * (2.0 / 8192)

    def split(table):
        high = table.astype(np.float32).astype(jnp.bfloat16)
        low = (table - high.astype(np.float64)).astype(np.float32).astype(jnp.bfloat16)
        return np.concatenate([high, high, low], 0)

    row_half = np.arange(8) // 4
    twiddle = np.zeros((BLOCKS, 2, 8, 128), np.float32)
    rowfix = np.zeros((BLOCKS, 2, 8, 128), np.float32)
    for index, k in enumerate(CLASSES):
        angle = -2 * np.pi * np.outer(k + 32 * row_half, lane) / 8192
        twiddle[index, 0], twiddle[index, 1] = np.cos(angle), np.sin(angle)
        angle = np.repeat((-2 * np.pi * k * row_half / 64)[:, None], 128, 1)
        rowfix[index, 0], rowfix[index, 1] = np.cos(angle), np.sin(angle)
    return split(forward), split(inverse), twiddle, rowfix


def add(a, b):
    return (a[0] + b[0], a[1] + b[1])


def sub(a, b):
    return (a[0] - b[0], a[1] - b[1])


def turn(a, step, period, sign):
    step = step % period
    if step == 0:
        return a
    if 4 * step == period:
        return (-a[1], a[0]) if sign > 0 else (a[1], -a[0])
    if 8 * step == period:
        r = np.float32(math.sqrt(0.5))
        if sign > 0:
            return ((a[0] - a[1]) * r, (a[0] + a[1]) * r)
        return ((a[0] + a[1]) * r, (a[1] - a[0]) * r)
    angle = sign * 2 * math.pi * step / period
    c, s = np.float32(math.cos(angle)), np.float32(math.sin(angle))
    return (a[0] * c - a[1] * s, a[0] * s + a[1] * c)


def small_dft(z, sign):
    n = len(z)
    if n == 1:
        return z
    even, odd = small_dft(z[0::2], sign), small_dft(z[1::2], sign)
    odd = [turn(value, j, n, sign) for j, value in enumerate(odd)]
    return [add(a, b) for a, b in zip(even, odd)] + [sub(a, b) for a, b in zip(even, odd)]


def blocks_forward(x):
    v = [x[c] + x[c + 8] for c in range(8)]
    u = [x[c] - x[c + 8] for c in range(8)]
    odd = small_dft([turn((x[c], -x[c + 8]), c, 32, -1) for c in range(8)], -1)
    two = small_dft([turn((u[c], -u[c + 4]), c, 16, -1) for c in range(4)], -1)
    a = [v[c] + v[c + 4] for c in range(4)]
    b = [v[c] - v[c + 4] for c in range(4)]
    four = small_dft([turn((b[c], -b[c + 2]), c, 8, -1) for c in range(2)], -1)
    e, o = a[0] + a[2], a[1] + a[3]
    eight = (a[0] - a[2], a[3] - a[1])
    return [(e + o, None), (e - o, None), eight] + four + two + odd


def blocks_inverse(spectrum):
    zero, sixteen, eight = spectrum[0], spectrum[1], spectrum[2]
    four, two, odd = spectrum[3:5], spectrum[5:9], spectrum[9:17]
    e, o = (zero[0] + sixteen[0]) * 0.5, (zero[0] - sixteen[0]) * 0.5
    a = [e + eight[0], o - eight[1], e - eight[0], o + eight[1]]
    g = [turn(value, c, 8, 1) for c, value in enumerate(small_dft(four, 1))]
    b = [g[0][0], g[1][0], -g[0][1], -g[1][1]]
    v = [a[c] + b[c] for c in range(4)] + [a[c] - b[c] for c in range(4)]
    g = [turn(value, c, 16, 1) for c, value in enumerate(small_dft(two, 1))]
    u = [value[0] for value in g] + [-value[1] for value in g]
    g = [turn(value, c, 32, 1) for c, value in enumerate(small_dft(odd, 1))]
    p = [v[c] + u[c] for c in range(8)]
    m = [v[c] - u[c] for c in range(8)]
    return [p[c] + g[c][0] for c in range(8)] + [m[c] - g[c][1] for c in range(8)]


def half_sign():
    rows = lax.broadcasted_iota(jnp.int32, (8, 128), 0)
    return jnp.where(rows < 4, 1.0, -1.0).astype(jnp.float32)


def swap_halves(a):
    return pltpu.roll(a, 4, 0)


def times(a, b, conjugate=False):
    if conjugate:
        return (a[0] * b[0] + a[1] * b[1], a[1] * b[0] - a[0] * b[1])
    return (a[0] * b[0] - a[1] * b[1], a[0] * b[1] + a[1] * b[0])


def butterfly(a, sign):
    return (a[0] * sign + swap_halves(a[0]), a[1] * sign + swap_halves(a[1]))


def multiply(source, target, table, start):
    block = source[start : start + 136, :]
    high = block.astype(jnp.bfloat16)
    low = (block - high.astype(jnp.float32)).astype(jnp.bfloat16)
    parts = jnp.concatenate([high, low, high], 1)
    target[start : start + 136, :] = jnp.dot(parts, table[...], preferred_element_type=jnp.float32)


def channel_bases():
    odd = lax.axis_index("zh") % 2
    return odd * 64, (1 - odd) * 64


def pack_kernel(value_hbm, key_hbm, query_hbm, cot_hbm, filter_hbm, out_ref, value_ref, key_ref, query_ref, cot_ref, filter_ref, sems):
    copies = [
        pltpu.make_async_copy(value_hbm, value_ref, sems.at[0]),
        pltpu.make_async_copy(key_hbm, key_ref, sems.at[1]),
        pltpu.make_async_copy(cot_hbm, cot_ref, sems.at[2]),
        pltpu.make_async_copy(query_hbm, query_ref, sems.at[3]),
    ]
    for copy in copies:
        copy.start()
    y, bases = lax.axis_index("y"), channel_bases()
    lanes = pl.ds(pl.multiple_of((y // 2) * 128, 128), 128)
    for core in range(2):
        rows = pl.ds(pl.multiple_of(bases[core] + (y % 2) * 32, 32), 32)
        copies.append(pltpu.make_async_copy(filter_hbm.at[rows, lanes], filter_ref.at[core], sems.at[4 + core]))
        copies[-1].start()
    places = [
        (core * 9 + half * 4 + j, pl.ds(pl.multiple_of(bases[core] + j * 32, 32), 32), pl.ds(half * 128, 128))
        for core in range(2)
        for j in range(2)
        for half in range(2)
    ]
    copies[0].wait()
    copies[1].wait()
    for at, rows, lanes in places:
        out_ref[pl.ds(at, 32, stride=18), :] = key_ref[rows, lanes] * value_ref[rows, lanes]
    copies[2].wait()
    copies[3].wait()
    for at, rows, lanes in places:
        out_ref[pl.ds(at + 2, 32, stride=18), :] = cot_ref[rows, lanes] * query_ref[rows, lanes]
    for core in range(2):
        copies[4 + core].wait()
        out_ref[pl.ds(core * 9 + 8, 32, stride=18), :] = filter_ref[core] * (1.0 / 64)


def spectrum_rows(blocks, scratch, base, sign, twiddle_ref, rowfix_ref):
    for index, value in enumerate(blocks_forward(blocks)):
        fix = (rowfix_ref[index, 0], rowfix_ref[index, 1])
        if value[1] is None:
            value = (value[0] * fix[0], value[0] * fix[1])
        else:
            value = times(value, fix)
        value = butterfly(value, sign)
        value = times(value, (twiddle_ref[index, 0], twiddle_ref[index, 1]))
        at = base + index * 8
        scratch[at : at + 8, 0:128] = value[0]
        scratch[at : at + 8, 128:256] = value[1]


def blocks_of(scratch, base, sign, twiddle_ref, rowfix_ref):
    spectrum = []
    for index in range(BLOCKS):
        at = base + index * 8
        value = (scratch[at : at + 8, 0:128], scratch[at : at + 8, 128:256])
        value = times(value, (twiddle_ref[index, 0], twiddle_ref[index, 1]), True)
        value = butterfly(value, sign)
        spectrum.append(times(value, (rowfix_ref[index, 0], rowfix_ref[index, 1]), True))
    return blocks_inverse(spectrum)


def forward_kernel(signal_ref, forward_ref, inverse_ref, twiddle_ref, rowfix_ref, spec_ref, part_ref, raw):
    sign = half_sign()
    for y in range(4):
        blocks = [signal_ref[(y * 16 + c) * 9 : (y * 16 + c) * 9 + 8, :] for c in range(16)]
        spectrum_rows(blocks, raw, y * 136, sign, twiddle_ref, rowfix_ref)
        multiply(raw, spec_ref, forward_ref, y * 136)
    for index in range(BLOCKS):
        total = None
        for y in range(4):
            at = y * 136 + index * 8
            value = (spec_ref[at : at + 8, 0:128], spec_ref[at : at + 8, 128:256])
            weight = (pltpu.roll(value[0], 6, 0), pltpu.roll(value[1], 6, 0))
            term = times(weight, value, True)
            total = term if total is None else add(total, term)
        raw[544 + index * 8 : 552 + index * 8, 0:128] = total[0]
        raw[544 + index * 8 : 552 + index * 8, 128:256] = total[1]
    multiply(raw, raw, inverse_ref, 544)
    blocks = blocks_of(raw, 544, sign, twiddle_ref, rowfix_ref)
    for c in range(16):
        for half in range(2):
            at = c * 4 + half * 2
            part_ref[at : at + 2, :] = blocks[c][half * 4 : half * 4 + 2, :]


def inverse_kernel(signal_ref, spec_ref, forward_ref, inverse_ref, twiddle_ref, rowfix_ref, out_ref, raw, spec, taps):
    sign = half_sign()
    for y in range(4):
        at = (y // 2) * 4 + y % 2
        for c in range(0, 16, 8):
            rows = signal_ref[pl.ds((y * 16 + c) * 9 + 8, 8, stride=9), :]
            taps[pl.ds(c * 8 + at, 8, stride=8), :] = rows
            taps[pl.ds(c * 8 + at + 2, 8, stride=8), :] = rows
    spectrum_rows([taps[c * 8 : c * 8 + 8, :] for c in range(16)], raw, 544, sign, twiddle_ref, rowfix_ref)
    multiply(raw, spec, forward_ref, 544)
    rows = lax.broadcasted_iota(jnp.int32, (8, 128), 0)
    flip = jnp.where(rows % 4 < 2, 1.0, -1.0).astype(jnp.float32)
    for y in range(4):
        for index in range(BLOCKS):
            at = 544 + index * 8
            tap = (spec[at : at + 8, 0:128], spec[at : at + 8, 128:256] * flip)
            at = y * 136 + index * 8
            value = times((spec_ref[at : at + 8, 0:128], spec_ref[at : at + 8, 128:256]), tap)
            raw[at : at + 8, 0:128] = value[0]
            raw[at : at + 8, 128:256] = value[1]
        multiply(raw, spec, inverse_ref, y * 136)
        blocks = blocks_of(spec, y * 136, sign, twiddle_ref, rowfix_ref)
        for c in range(16):
            at = (y * 16 + c) * 12
            out_ref[at : at + 8, :] = blocks[c]


def filter_kernel(part_ref, *refs):
    *more_refs, message_ref, out_ref = refs
    out_ref[...] = message_ref[...]
    for c in range(0, 16, 2):
        pair = part_ref[c * 4 : c * 4 + 8, :]
        for more in more_refs:
            pair = pair + more[c * 4 : c * 4 + 8, :]
        pair = pair * (1.0 / 64)
        for y in range(4):
            at = (y * 16 + c) * 12
            out_ref[at + 8 : at + 12, :] = pair[0:4, :]
            out_ref[at + 20 : at + 24, :] = pair[4:8, :]


def unpack_kernel(signal_ref, value_ref, key_ref, cot_ref, query_out, key_out, value_out, filter_out):
    bases = channel_bases()
    for core in range(2):
        for j in range(2):
            rows = pl.ds(pl.multiple_of(bases[core] + j * 32, 32), 32)
            for half in range(2):
                lanes = pl.ds(half * 128, 128)
                at = core * 12 + half * 4 + j
                conv = signal_ref[pl.ds(at, 32, stride=24), :]
                grad = signal_ref[pl.ds(at + 2, 32, stride=24), :]
                query_out[rows, lanes] = cot_ref[rows, lanes] * conv
                key_out[rows, lanes] = grad * value_ref[rows, lanes]
                value_out[rows, lanes] = grad * key_ref[rows, lanes]
                filter_out[rows, lanes] = signal_ref[pl.ds(core * 12 + 8 + half * 2 + j, 32, stride=24), :]


def call(kernel, shapes, inputs, scratch=(), copies=0, **extra):
    return pl.pallas_call(
        kernel,
        out_shape=[jax.ShapeDtypeStruct(shape, jnp.float32) for shape in shapes],
        in_specs=[HBM if copies else VMEM] * inputs,
        out_specs=[VMEM] * len(shapes),
        scratch_shapes=[pltpu.VMEM(shape, jnp.float32) for shape in scratch]
        + ([pltpu.SemaphoreType.DMA((copies,))] if copies else []),
        compiler_params=PARAMS,
        **extra,
    )


def exchange(array, axes):
    return lax.all_to_all(array, axes, split_axis=0, concat_axis=0, tiled=True)


def on_device(value_in, key_in, query_in, cotangent, filter_param):
    value_in, key_in, query_in, cotangent = value_in[0], key_in[0], query_in[0], cotangent[0]
    forward, inverse, twiddle, rowfix = [jnp.asarray(table) for table in tables()]
    pinned = [pltpu.with_memory_space_constraint(a, pltpu.HBM) for a in (value_in, key_in, query_in, cotangent, filter_param)]
    (message,) = call(pack_kernel, [(576, 128)], 5, [(128, 256)] * 4 + [(2, 32, 128)], copies=6)(
        *pinned
    )
    signal = exchange(message.reshape(64, 1, 1152), FAR).reshape(576, 128)
    spec, part = call(forward_kernel, [(544, 256), (64, 128)], 5, [(680, 256)])(
        signal, forward, inverse, twiddle, rowfix
    )
    for pairs in STEPS:
        part = part + lax.ppermute(part, ("zh", "core"), pairs)
    (message,) = call(inverse_kernel, [(768, 128)], 6, [(680, 256)] * 2 + [(128, 128)])(
        signal, spec, forward, inverse, twiddle, rowfix
    )
    (message,) = call(filter_kernel, [(768, 128)], 2)(part, message)
    signal = exchange(message.reshape(64, 1, 1536), FAR).reshape(768, 128)
    shape = (128, 256)
    query_grad, key_grad, value_grad, filter_grad = call(unpack_kernel, [shape] * 4, 4)(
        signal, value_in, key_in, cotangent
    )
    return query_grad[None], key_grad[None], value_grad[None], filter_grad


def solution(mesh):
    fine = Mesh(mesh.devices.reshape(4, 4, 4, 2, 2), AXES)
    signal = P(("zh", "y"), None, ("x", "zl", "core"))
    taps = P(None, ("x", "zl", "core"))
    return jax.shard_map(
        on_device,
        mesh=fine,
        in_specs=(signal, signal, signal, signal, taps),
        out_specs=(signal, signal, signal, taps),
        check_vma=False,
    )
```

```python
import math

import jax
import jax.numpy as jnp
import numpy as np
from jax import lax
from jax.experimental import pallas as pl
from jax.experimental.pallas import tpu as pltpu
from jax.sharding import Mesh, PartitionSpec as P

AXES = ("zh", "y", "x", "zl", "core")
ORDERS = ((3, 2, 1, 0), (1, 0, 3, 2))
STEPS = [
    [
        (2 * zh + core, 2 * ORDERS[(step + core + zh) % 2][zh] + 1 - core)
        for zh in range(4)
        for core in range(2)
    ]
    for step in range(2)
]
FAR = ("zl", "x", "y", "core")
BLOCKS = 17
CLASSES = [0, 16, 8, 4, 20] + [8 * j + 2 for j in range(4)] + [4 * j + 1 for j in range(8)]
VMEM = pl.BlockSpec(memory_space=pltpu.VMEM)
HBM = pl.BlockSpec(memory_space=pltpu.HBM)
PARAMS = pltpu.CompilerParams(vmem_limit_bytes=48 * 1024 * 1024)


def tables():
    lane = np.arange(128)
    forward = np.zeros((256, 256))
    angle = 2 * np.pi * np.outer(lane, lane) / 128
    c, s = np.cos(angle), np.sin(angle)
    forward = np.block([[c, -s], [s, c]])
    inverse = np.block([[c, s], [-s, c]]) * (2.0 / 8192)

    def split(table):
        high = table.astype(np.float32).astype(jnp.bfloat16)
        low = (table - high.astype(np.float64)).astype(np.float32).astype(jnp.bfloat16)
        return np.concatenate([high, high, low], 0)

    row_half = np.arange(8) // 4
    twiddle = np.zeros((BLOCKS, 2, 8, 128), np.float32)
    rowfix = np.zeros((BLOCKS, 2, 8, 128), np.float32)
    for index, k in enumerate(CLASSES):
        angle = -2 * np.pi * np.outer(k + 32 * row_half, lane) / 8192
        twiddle[index, 0], twiddle[index, 1] = np.cos(angle), np.sin(angle)
        angle = np.repeat((-2 * np.pi * k * row_half / 64)[:, None], 128, 1)
        rowfix[index, 0], rowfix[index, 1] = np.cos(angle), np.sin(angle)
    return split(forward), split(inverse), twiddle, rowfix


def add(a, b):
    return (a[0] + b[0], a[1] + b[1])


def sub(a, b):
    return (a[0] - b[0], a[1] - b[1])


def turn(a, step, period, sign):
    step = step % period
    if step == 0:
        return a
    if 4 * step == period:
        return (-a[1], a[0]) if sign > 0 else (a[1], -a[0])
    if 8 * step == period:
        r = np.float32(math.sqrt(0.5))
        if sign > 0:
            return ((a[0] - a[1]) * r, (a[0] + a[1]) * r)
        return ((a[0] + a[1]) * r, (a[1] - a[0]) * r)
    angle = sign * 2 * math.pi * step / period
    c, s = np.float32(math.cos(angle)), np.float32(math.sin(angle))
    return (a[0] * c - a[1] * s, a[0] * s + a[1] * c)


def small_dft(z, sign):
    n = len(z)
    if n == 1:
        return z
    even, odd = small_dft(z[0::2], sign), small_dft(z[1::2], sign)
    odd = [turn(value, j, n, sign) for j, value in enumerate(odd)]
    return [add(a, b) for a, b in zip(even, odd)] + [sub(a, b) for a, b in zip(even, odd)]


def blocks_forward(x):
    v = [x[c] + x[c + 8] for c in range(8)]
    u = [x[c] - x[c + 8] for c in range(8)]
    odd = small_dft([turn((x[c], -x[c + 8]), c, 32, -1) for c in range(8)], -1)
    two = small_dft([turn((u[c], -u[c + 4]), c, 16, -1) for c in range(4)], -1)
    a = [v[c] + v[c + 4] for c in range(4)]
    b = [v[c] - v[c + 4] for c in range(4)]
    four = small_dft([turn((b[c], -b[c + 2]), c, 8, -1) for c in range(2)], -1)
    e, o = a[0] + a[2], a[1] + a[3]
    eight = (a[0] - a[2], a[3] - a[1])
    return [(e + o, None), (e - o, None), eight] + four + two + odd


def blocks_inverse(spectrum):
    zero, sixteen, eight = spectrum[0], spectrum[1], spectrum[2]
    four, two, odd = spectrum[3:5], spectrum[5:9], spectrum[9:17]
    e, o = (zero[0] + sixteen[0]) * 0.5, (zero[0] - sixteen[0]) * 0.5
    a = [e + eight[0], o - eight[1], e - eight[0], o + eight[1]]
    g = [turn(value, c, 8, 1) for c, value in enumerate(small_dft(four, 1))]
    b = [g[0][0], g[1][0], -g[0][1], -g[1][1]]
    v = [a[c] + b[c] for c in range(4)] + [a[c] - b[c] for c in range(4)]
    g = [turn(value, c, 16, 1) for c, value in enumerate(small_dft(two, 1))]
    u = [value[0] for value in g] + [-value[1] for value in g]
    g = [turn(value, c, 32, 1) for c, value in enumerate(small_dft(odd, 1))]
    p = [v[c] + u[c] for c in range(8)]
    m = [v[c] - u[c] for c in range(8)]
    return [p[c] + g[c][0] for c in range(8)] + [m[c] - g[c][1] for c in range(8)]


def half_sign():
    rows = lax.broadcasted_iota(jnp.int32, (8, 128), 0)
    return jnp.where(rows < 4, 1.0, -1.0).astype(jnp.float32)


def swap_halves(a):
    return pltpu.roll(a, 4, 0)


def times(a, b, conjugate=False):
    if conjugate:
        return (a[0] * b[0] + a[1] * b[1], a[1] * b[0] - a[0] * b[1])
    return (a[0] * b[0] - a[1] * b[1], a[0] * b[1] + a[1] * b[0])


def butterfly(a, sign):
    return (a[0] * sign + swap_halves(a[0]), a[1] * sign + swap_halves(a[1]))


def multiply(source, target, table, start):
    block = source[start : start + 136, :]
    high = block.astype(jnp.bfloat16)
    low = (block - high.astype(jnp.float32)).astype(jnp.bfloat16)
    parts = jnp.concatenate([high, low, high], 1)
    target[start : start + 136, :] = jnp.dot(parts, table[...], preferred_element_type=jnp.float32)


def channel_bases():
    odd = lax.axis_index("zh") % 2
    return odd * 64, (1 - odd) * 64


def pack_kernel(value_hbm, key_hbm, query_hbm, cot_hbm, filter_hbm, out_ref, value_ref, key_ref, query_ref, cot_ref, filter_ref, sems):
    copies = [
        pltpu.make_async_copy(value_hbm, value_ref, sems.at[0]),
        pltpu.make_async_copy(key_hbm, key_ref, sems.at[1]),
        pltpu.make_async_copy(cot_hbm, cot_ref, sems.at[2]),
        pltpu.make_async_copy(query_hbm, query_ref, sems.at[3]),
    ]
    for copy in copies:
        copy.start()
    y, bases = lax.axis_index("y"), channel_bases()
    lanes = pl.ds(pl.multiple_of((y // 2) * 128, 128), 128)
    for core in range(2):
        rows = pl.ds(pl.multiple_of(bases[core] + (y % 2) * 32, 32), 32)
        copies.append(pltpu.make_async_copy(filter_hbm.at[rows, lanes], filter_ref.at[core], sems.at[4 + core]))
        copies[-1].start()
    places = [
        (core * 9 + half * 4 + j, pl.ds(pl.multiple_of(bases[core] + j * 32, 32), 32), pl.ds(half * 128, 128))
        for core in range(2)
        for j in range(2)
        for half in range(2)
    ]
    copies[0].wait()
    copies[1].wait()
    for at, rows, lanes in places:
        out_ref[pl.ds(at, 32, stride=18), :] = key_ref[rows, lanes] * value_ref[rows, lanes]
    copies[2].wait()
    copies[3].wait()
    for at, rows, lanes in places:
        out_ref[pl.ds(at + 2, 32, stride=18), :] = cot_ref[rows, lanes] * query_ref[rows, lanes]
    for core in range(2):
        copies[4 + core].wait()
        out_ref[pl.ds(core * 9 + 8, 32, stride=18), :] = filter_ref[core] * (1.0 / 64)


def place(y, c):
    return (c // 2 % 2) * 32 + (c // 4) * 8 + y * 2 + c % 2


def spectrum_rows(blocks, scratch, base, sign, twiddle_ref, rowfix_ref):
    for index, value in enumerate(blocks_forward(blocks)):
        fix = (rowfix_ref[index, 0], rowfix_ref[index, 1])
        if value[1] is None:
            value = (value[0] * fix[0], value[0] * fix[1])
        else:
            value = times(value, fix)
        value = butterfly(value, sign)
        value = times(value, (twiddle_ref[index, 0], twiddle_ref[index, 1]))
        at = base + index * 8
        scratch[at : at + 8, 0:128] = value[0]
        scratch[at : at + 8, 128:256] = value[1]


def blocks_of(scratch, base, sign, twiddle_ref, rowfix_ref):
    spectrum = []
    for index in range(BLOCKS):
        at = base + index * 8
        value = (scratch[at : at + 8, 0:128], scratch[at : at + 8, 128:256])
        value = times(value, (twiddle_ref[index, 0], twiddle_ref[index, 1]), True)
        value = butterfly(value, sign)
        spectrum.append(times(value, (rowfix_ref[index, 0], rowfix_ref[index, 1]), True))
    return blocks_inverse(spectrum)


def forward_kernel(signal_ref, forward_ref, inverse_ref, twiddle_ref, rowfix_ref, spec_ref, part_ref, raw):
    sign = half_sign()
    for y in range(4):
        blocks = [signal_ref[place(y, c) * 9 : place(y, c) * 9 + 8, :] for c in range(16)]
        spectrum_rows(blocks, raw, y * 136, sign, twiddle_ref, rowfix_ref)
        multiply(raw, spec_ref, forward_ref, y * 136)
    for index in range(BLOCKS):
        total = None
        for y in range(4):
            at = y * 136 + index * 8
            value = (spec_ref[at : at + 8, 0:128], spec_ref[at : at + 8, 128:256])
            weight = (pltpu.roll(value[0], 6, 0), pltpu.roll(value[1], 6, 0))
            term = times(weight, value, True)
            total = term if total is None else add(total, term)
        raw[544 + index * 8 : 552 + index * 8, 0:128] = total[0]
        raw[544 + index * 8 : 552 + index * 8, 128:256] = total[1]
    multiply(raw, raw, inverse_ref, 544)
    blocks = blocks_of(raw, 544, sign, twiddle_ref, rowfix_ref)
    for c in range(16):
        for half in range(2):
            at = c * 4 + half * 2
            part_ref[at : at + 2, :] = blocks[c][half * 4 : half * 4 + 2, :]


def inverse_kernel(signal_ref, spec_ref, forward_ref, inverse_ref, twiddle_ref, rowfix_ref, out_ref, raw, spec, taps):
    sign = half_sign()
    for y in range(4):
        at = (y // 2) * 4 + y % 2
        for c in range(4):
            rows = signal_ref[pl.ds(place(y, c) * 9 + 8, 4, stride=72), :]
            taps[pl.ds(c * 8 + at, 4, stride=32), :] = rows
            taps[pl.ds(c * 8 + at + 2, 4, stride=32), :] = rows
    spectrum_rows([taps[c * 8 : c * 8 + 8, :] for c in range(16)], raw, 544, sign, twiddle_ref, rowfix_ref)
    multiply(raw, spec, forward_ref, 544)
    rows = lax.broadcasted_iota(jnp.int32, (8, 128), 0)
    flip = jnp.where(rows % 4 < 2, 1.0, -1.0).astype(jnp.float32)
    for y in range(4):
        for index in range(BLOCKS):
            at = 544 + index * 8
            tap = (spec[at : at + 8, 0:128], spec[at : at + 8, 128:256] * flip)
            at = y * 136 + index * 8
            value = times((spec_ref[at : at + 8, 0:128], spec_ref[at : at + 8, 128:256]), tap)
            raw[at : at + 8, 0:128] = value[0]
            raw[at : at + 8, 128:256] = value[1]
        multiply(raw, spec, inverse_ref, y * 136)
        blocks = blocks_of(spec, y * 136, sign, twiddle_ref, rowfix_ref)
        for c in range(16):
            at = place(y, c) * 12
            out_ref[at : at + 8, :] = blocks[c]


def filter_kernel(part_ref, *refs):
    *more_refs, message_ref, out_ref = refs
    out_ref[...] = message_ref[...]
    for c in range(0, 16, 2):
        pair = part_ref[c * 4 : c * 4 + 8, :]
        for more in more_refs:
            pair = pair + more[c * 4 : c * 4 + 8, :]
        pair = pair * (1.0 / 64)
        for y in range(4):
            at = place(y, c) * 12
            out_ref[at + 8 : at + 12, :] = pair[0:4, :]
            out_ref[at + 20 : at + 24, :] = pair[4:8, :]


def unpack_kernel(signal_ref, value_ref, key_ref, cot_ref, query_out, key_out, value_out, filter_out):
    bases = channel_bases()
    for core in range(2):
        for j in range(2):
            rows = pl.ds(pl.multiple_of(bases[core] + j * 32, 32), 32)
            for half in range(2):
                lanes = pl.ds(half * 128, 128)
                at = core * 12 + half * 4 + j
                conv = signal_ref[pl.ds(at, 32, stride=24), :]
                grad = signal_ref[pl.ds(at + 2, 32, stride=24), :]
                query_out[rows, lanes] = cot_ref[rows, lanes] * conv
                key_out[rows, lanes] = grad * value_ref[rows, lanes]
                value_out[rows, lanes] = grad * key_ref[rows, lanes]
                filter_out[rows, lanes] = signal_ref[pl.ds(core * 12 + 8 + half * 2 + j, 32, stride=24), :]


def call(kernel, shapes, inputs, scratch=(), copies=0, **extra):
    return pl.pallas_call(
        kernel,
        out_shape=[jax.ShapeDtypeStruct(shape, jnp.float32) for shape in shapes],
        in_specs=[HBM if copies else VMEM] * inputs,
        out_specs=[VMEM] * len(shapes),
        scratch_shapes=[pltpu.VMEM(shape, jnp.float32) for shape in scratch]
        + ([pltpu.SemaphoreType.DMA((copies,))] if copies else []),
        compiler_params=PARAMS,
        **extra,
    )


def exchange(array, axes):
    return lax.all_to_all(array, axes, split_axis=0, concat_axis=0, tiled=True)


def on_device(value_in, key_in, query_in, cotangent, filter_param):
    value_in, key_in, query_in, cotangent = value_in[0], key_in[0], query_in[0], cotangent[0]
    forward, inverse, twiddle, rowfix = [jnp.asarray(table) for table in tables()]
    pinned = [pltpu.with_memory_space_constraint(a, pltpu.HBM) for a in (value_in, key_in, query_in, cotangent, filter_param)]
    (message,) = call(pack_kernel, [(576, 128)], 5, [(128, 256)] * 4 + [(2, 32, 128)], copies=6)(
        *pinned
    )
    signal = exchange(message.reshape(64, 1, 1152), FAR).reshape(576, 128)
    spec, part = call(forward_kernel, [(544, 256), (64, 128)], 5, [(680, 256)])(
        signal, forward, inverse, twiddle, rowfix
    )
    for pairs in STEPS:
        part = part + lax.ppermute(part, ("zh", "core"), pairs)
    (message,) = call(inverse_kernel, [(768, 128)], 6, [(680, 256)] * 2 + [(128, 128)])(
        signal, spec, forward, inverse, twiddle, rowfix
    )
    (message,) = call(filter_kernel, [(768, 128)], 2)(part, message)
    signal = exchange(message.reshape(64, 1, 1536), FAR).reshape(768, 128)
    shape = (128, 256)
    query_grad, key_grad, value_grad, filter_grad = call(unpack_kernel, [shape] * 4, 4)(
        signal, value_in, key_in, cotangent
    )
    return query_grad[None], key_grad[None], value_grad[None], filter_grad


def solution(mesh):
    fine = Mesh(mesh.devices.reshape(4, 4, 4, 2, 2), AXES)
    signal = P(("zh", "y"), None, ("x", "zl", "core"))
    taps = P(None, ("x", "zl", "core"))
    return jax.shard_map(
        on_device,
        mesh=fine,
        in_specs=(signal, signal, signal, signal, taps),
        out_specs=(signal, signal, signal, taps),
        check_vma=False,
    )
```

```python
import math

import jax
import jax.numpy as jnp
import numpy as np
from jax import lax
from jax.experimental import pallas as pl
from jax.experimental.pallas import tpu as pltpu
from jax.sharding import Mesh, PartitionSpec as P

AXES = ("zh", "y", "x", "zl", "core")
ORDERS = ((3, 2, 1, 0), (1, 0, 3, 2))
STEPS = [
    [
        (2 * zh + core, 2 * ORDERS[(step + core + zh) % 2][zh] + 1 - core)
        for zh in range(4)
        for core in range(2)
    ]
    for step in range(2)
]
FAR = ("zl", "x", "y", "core")
BLOCKS = 17
CLASSES = [0, 16, 8, 4, 20] + [8 * j + 2 for j in range(4)] + [4 * j + 1 for j in range(8)]
VMEM = pl.BlockSpec(memory_space=pltpu.VMEM)
HBM = pl.BlockSpec(memory_space=pltpu.HBM)
PARAMS = pltpu.CompilerParams(vmem_limit_bytes=48 * 1024 * 1024)


def tables():
    lane = np.arange(128)
    forward = np.zeros((256, 256))
    angle = 2 * np.pi * np.outer(lane, lane) / 128
    c, s = np.cos(angle), np.sin(angle)
    forward = np.block([[c, -s], [s, c]])
    inverse = np.block([[c, s], [-s, c]]) * (2.0 / 8192)

    def split(table):
        high = table.astype(np.float32).astype(jnp.bfloat16)
        low = (table - high.astype(np.float64)).astype(np.float32).astype(jnp.bfloat16)
        return np.concatenate([high, high, low], 0)

    row_half = np.arange(8) // 4
    twiddle = np.zeros((BLOCKS, 2, 8, 128), np.float32)
    rowfix = np.zeros((BLOCKS, 2, 8, 128), np.float32)
    for index, k in enumerate(CLASSES):
        angle = -2 * np.pi * np.outer(k + 32 * row_half, lane) / 8192
        twiddle[index, 0], twiddle[index, 1] = np.cos(angle), np.sin(angle)
        angle = np.repeat((-2 * np.pi * k * row_half / 64)[:, None], 128, 1)
        rowfix[index, 0], rowfix[index, 1] = np.cos(angle), np.sin(angle)
    return split(forward), split(inverse), twiddle, rowfix


def add(a, b):
    return (a[0] + b[0], a[1] + b[1])


def sub(a, b):
    return (a[0] - b[0], a[1] - b[1])


def turn(a, step, period, sign):
    step = step % period
    if step == 0:
        return a
    if 4 * step == period:
        return (-a[1], a[0]) if sign > 0 else (a[1], -a[0])
    if 8 * step == period:
        r = np.float32(math.sqrt(0.5))
        if sign > 0:
            return ((a[0] - a[1]) * r, (a[0] + a[1]) * r)
        return ((a[0] + a[1]) * r, (a[1] - a[0]) * r)
    angle = sign * 2 * math.pi * step / period
    c, s = np.float32(math.cos(angle)), np.float32(math.sin(angle))
    return (a[0] * c - a[1] * s, a[0] * s + a[1] * c)


def small_dft(z, sign):
    n = len(z)
    if n == 1:
        return z
    even, odd = small_dft(z[0::2], sign), small_dft(z[1::2], sign)
    odd = [turn(value, j, n, sign) for j, value in enumerate(odd)]
    return [add(a, b) for a, b in zip(even, odd)] + [sub(a, b) for a, b in zip(even, odd)]


def blocks_forward(x):
    v = [x[c] + x[c + 8] for c in range(8)]
    u = [x[c] - x[c + 8] for c in range(8)]
    odd = small_dft([turn((x[c], -x[c + 8]), c, 32, -1) for c in range(8)], -1)
    two = small_dft([turn((u[c], -u[c + 4]), c, 16, -1) for c in range(4)], -1)
    a = [v[c] + v[c + 4] for c in range(4)]
    b = [v[c] - v[c + 4] for c in range(4)]
    four = small_dft([turn((b[c], -b[c + 2]), c, 8, -1) for c in range(2)], -1)
    e, o = a[0] + a[2], a[1] + a[3]
    eight = (a[0] - a[2], a[3] - a[1])
    return [(e + o, None), (e - o, None), eight] + four + two + odd


def blocks_inverse(spectrum):
    zero, sixteen, eight = spectrum[0], spectrum[1], spectrum[2]
    four, two, odd = spectrum[3:5], spectrum[5:9], spectrum[9:17]
    e, o = (zero[0] + sixteen[0]) * 0.5, (zero[0] - sixteen[0]) * 0.5
    a = [e + eight[0], o - eight[1], e - eight[0], o + eight[1]]
    g = [turn(value, c, 8, 1) for c, value in enumerate(small_dft(four, 1))]
    b = [g[0][0], g[1][0], -g[0][1], -g[1][1]]
    v = [a[c] + b[c] for c in range(4)] + [a[c] - b[c] for c in range(4)]
    g = [turn(value, c, 16, 1) for c, value in enumerate(small_dft(two, 1))]
    u = [value[0] for value in g] + [-value[1] for value in g]
    g = [turn(value, c, 32, 1) for c, value in enumerate(small_dft(odd, 1))]
    p = [v[c] + u[c] for c in range(8)]
    m = [v[c] - u[c] for c in range(8)]
    return [p[c] + g[c][0] for c in range(8)] + [m[c] - g[c][1] for c in range(8)]


def half_sign():
    rows = lax.broadcasted_iota(jnp.int32, (8, 128), 0)
    return jnp.where(rows < 4, 1.0, -1.0).astype(jnp.float32)


def swap_halves(a):
    return pltpu.roll(a, 4, 0)


def times(a, b, conjugate=False):
    if conjugate:
        return (a[0] * b[0] + a[1] * b[1], a[1] * b[0] - a[0] * b[1])
    return (a[0] * b[0] - a[1] * b[1], a[0] * b[1] + a[1] * b[0])


def butterfly(a, sign):
    return (a[0] * sign + swap_halves(a[0]), a[1] * sign + swap_halves(a[1]))


def multiply(source, target, table, start):
    block = source[start : start + 136, :]
    high = block.astype(jnp.bfloat16)
    low = (block - high.astype(jnp.float32)).astype(jnp.bfloat16)
    parts = jnp.concatenate([high, low, high], 1)
    target[start : start + 136, :] = jnp.dot(parts, table[...], preferred_element_type=jnp.float32)


def channel_bases():
    odd = lax.axis_index("zh") % 2
    return odd * 64, (1 - odd) * 64


def pack_kernel(value_hbm, key_hbm, query_hbm, cot_hbm, filter_hbm, out_ref, value_ref, key_ref, cot_ref, query_ref, filter_ref, sems):
    copies = [
        pltpu.make_async_copy(value_hbm, value_ref, sems.at[0]),
        pltpu.make_async_copy(key_hbm, key_ref, sems.at[1]),
        pltpu.make_async_copy(cot_hbm, cot_ref, sems.at[2]),
        pltpu.make_async_copy(query_hbm, query_ref, sems.at[3]),
    ]
    for copy in copies:
        copy.start()
    y, bases = lax.axis_index("y"), channel_bases()
    lanes = pl.ds(pl.multiple_of((y // 2) * 128, 128), 128)
    for core in range(2):
        rows = pl.ds(pl.multiple_of(bases[core] + (y % 2) * 32, 32), 32)
        copies.append(pltpu.make_async_copy(filter_hbm.at[rows, lanes], filter_ref.at[core], sems.at[4 + core]))
        copies[-1].start()
    places = [
        (core * 9 + half * 4 + j, pl.ds(pl.multiple_of(bases[core] + j * 32, 32), 32), pl.ds(half * 128, 128))
        for core in range(2)
        for j in range(2)
        for half in range(2)
    ]
    copies[0].wait()
    copies[1].wait()
    for at, rows, lanes in places:
        out_ref[pl.ds(at, 32, stride=18), :] = key_ref[rows, lanes] * value_ref[rows, lanes]
    copies[2].wait()
    copies[3].wait()
    for at, rows, lanes in places:
        out_ref[pl.ds(at + 2, 32, stride=18), :] = cot_ref[rows, lanes] * query_ref[rows, lanes]
    for core in range(2):
        copies[4 + core].wait()
        out_ref[pl.ds(core * 9 + 8, 32, stride=18), :] = filter_ref[core] * (1.0 / 64)


def place(y, c):
    return (c // 2 % 2) * 32 + (c // 4) * 8 + y * 2 + c % 2


def spectrum_rows(blocks, scratch, base, sign, twiddle_ref, rowfix_ref):
    for index, value in enumerate(blocks_forward(blocks)):
        fix = (rowfix_ref[index, 0], rowfix_ref[index, 1])
        if value[1] is None:
            value = (value[0] * fix[0], value[0] * fix[1])
        else:
            value = times(value, fix)
        value = butterfly(value, sign)
        value = times(value, (twiddle_ref[index, 0], twiddle_ref[index, 1]))
        at = base + index * 8
        scratch[at : at + 8, 0:128] = value[0]
        scratch[at : at + 8, 128:256] = value[1]


def blocks_of(scratch, base, sign, twiddle_ref, rowfix_ref):
    spectrum = []
    for index in range(BLOCKS):
        at = base + index * 8
        value = (scratch[at : at + 8, 0:128], scratch[at : at + 8, 128:256])
        value = times(value, (twiddle_ref[index, 0], twiddle_ref[index, 1]), True)
        value = butterfly(value, sign)
        spectrum.append(times(value, (rowfix_ref[index, 0], rowfix_ref[index, 1]), True))
    return blocks_inverse(spectrum)


def forward_kernel(signal_ref, forward_ref, inverse_ref, twiddle_ref, rowfix_ref, spec_ref, part_ref, raw):
    sign = half_sign()
    for y in range(4):
        blocks = [signal_ref[place(y, c) * 9 : place(y, c) * 9 + 8, :] for c in range(16)]
        spectrum_rows(blocks, raw, y * 136, sign, twiddle_ref, rowfix_ref)
        multiply(raw, spec_ref, forward_ref, y * 136)
    for index in range(BLOCKS):
        total = None
        for y in range(4):
            at = y * 136 + index * 8
            value = (spec_ref[at : at + 8, 0:128], spec_ref[at : at + 8, 128:256])
            weight = (pltpu.roll(value[0], 6, 0), pltpu.roll(value[1], 6, 0))
            term = times(weight, value, True)
            total = term if total is None else add(total, term)
        raw[544 + index * 8 : 552 + index * 8, 0:128] = total[0]
        raw[544 + index * 8 : 552 + index * 8, 128:256] = total[1]
    multiply(raw, raw, inverse_ref, 544)
    blocks = blocks_of(raw, 544, sign, twiddle_ref, rowfix_ref)
    for c in range(16):
        for half in range(2):
            at = c * 4 + half * 2
            part_ref[at : at + 2, :] = blocks[c][half * 4 : half * 4 + 2, :]


def inverse_kernel(signal_ref, spec_ref, forward_ref, inverse_ref, twiddle_ref, rowfix_ref, out_ref, raw, spec, taps):
    sign = half_sign()
    for y in range(4):
        at = (y // 2) * 4 + y % 2
        for c in range(4):
            rows = signal_ref[pl.ds(place(y, c) * 9 + 8, 4, stride=72), :]
            taps[pl.ds(c * 8 + at, 4, stride=32), :] = rows
            taps[pl.ds(c * 8 + at + 2, 4, stride=32), :] = rows
    spectrum_rows([taps[c * 8 : c * 8 + 8, :] for c in range(16)], raw, 544, sign, twiddle_ref, rowfix_ref)
    multiply(raw, spec, forward_ref, 544)
    rows = lax.broadcasted_iota(jnp.int32, (8, 128), 0)
    flip = jnp.where(rows % 4 < 2, 1.0, -1.0).astype(jnp.float32)
    for y in range(4):
        for index in range(BLOCKS):
            at = 544 + index * 8
            tap = (spec[at : at + 8, 0:128], spec[at : at + 8, 128:256] * flip)
            at = y * 136 + index * 8
            value = times((spec_ref[at : at + 8, 0:128], spec_ref[at : at + 8, 128:256]), tap)
            raw[at : at + 8, 0:128] = value[0]
            raw[at : at + 8, 128:256] = value[1]
        multiply(raw, spec, inverse_ref, y * 136)
        blocks = blocks_of(spec, y * 136, sign, twiddle_ref, rowfix_ref)
        for c in range(16):
            at = place(y, c) * 12
            out_ref[at : at + 8, :] = blocks[c]


def filter_kernel(part_ref, *refs):
    *more_refs, message_ref, out_ref = refs
    out_ref[...] = message_ref[...]
    for c in range(0, 16, 2):
        pair = part_ref[c * 4 : c * 4 + 8, :]
        for more in more_refs:
            pair = pair + more[c * 4 : c * 4 + 8, :]
        pair = pair * (1.0 / 64)
        for y in range(4):
            at = place(y, c) * 12
            out_ref[at + 8 : at + 12, :] = pair[0:4, :]
            out_ref[at + 20 : at + 24, :] = pair[4:8, :]


def unpack_kernel(signal_ref, value_ref, key_ref, cot_ref, query_out, key_out, value_out, filter_out):
    bases = channel_bases()
    for core in range(2):
        for j in range(2):
            rows = pl.ds(pl.multiple_of(bases[core] + j * 32, 32), 32)
            for half in range(2):
                lanes = pl.ds(half * 128, 128)
                at = core * 12 + half * 4 + j
                conv = signal_ref[pl.ds(at, 32, stride=24), :]
                grad = signal_ref[pl.ds(at + 2, 32, stride=24), :]
                query_out[rows, lanes] = cot_ref[rows, lanes] * conv
                key_out[rows, lanes] = grad * value_ref[rows, lanes]
                value_out[rows, lanes] = grad * key_ref[rows, lanes]
                filter_out[rows, lanes] = signal_ref[pl.ds(core * 12 + 8 + half * 2 + j, 32, stride=24), :]


def call(kernel, shapes, inputs, scratch=(), copies=0, **extra):
    return pl.pallas_call(
        kernel,
        out_shape=[jax.ShapeDtypeStruct(shape, jnp.float32) for shape in shapes],
        in_specs=[HBM if copies else VMEM] * inputs,
        out_specs=[VMEM] * len(shapes),
        scratch_shapes=[pltpu.VMEM(shape, jnp.float32) for shape in scratch]
        + ([pltpu.SemaphoreType.DMA((copies,))] if copies else []),
        compiler_params=PARAMS,
        **extra,
    )


def exchange(array, axes):
    return lax.all_to_all(array, axes, split_axis=0, concat_axis=0, tiled=True)


def on_device(value_in, key_in, query_in, cotangent, filter_param):
    value_in, key_in, query_in, cotangent = value_in[0], key_in[0], query_in[0], cotangent[0]
    forward, inverse, twiddle, rowfix = [jnp.asarray(table) for table in tables()]
    pinned = [pltpu.with_memory_space_constraint(a, pltpu.HBM) for a in (value_in, key_in, query_in, cotangent, filter_param)]
    shape = (128, 256)
    message, value, key, cot = call(pack_kernel, [(576, 128)] + [shape] * 3, 5, [shape, (2, 32, 128)], copies=6)(*pinned)
    signal = exchange(message.reshape(64, 1, 1152), FAR).reshape(576, 128)
    spec, part = call(forward_kernel, [(544, 256), (64, 128)], 5, [(680, 256)])(
        signal, forward, inverse, twiddle, rowfix
    )
    for pairs in STEPS:
        part = part + lax.ppermute(part, ("zh", "core"), pairs)
    (message,) = call(inverse_kernel, [(768, 128)], 6, [(680, 256)] * 2 + [(128, 128)])(
        signal, spec, forward, inverse, twiddle, rowfix
    )
    (message,) = call(filter_kernel, [(768, 128)], 2)(part, message)
    signal = exchange(message.reshape(64, 1, 1536), FAR).reshape(768, 128)
    query_grad, key_grad, value_grad, filter_grad = call(unpack_kernel, [shape] * 4, 4)(signal, value, key, cot)
    return query_grad[None], key_grad[None], value_grad[None], filter_grad


def solution(mesh):
    fine = Mesh(mesh.devices.reshape(4, 4, 4, 2, 2), AXES)
    signal = P(("zh", "y"), None, ("x", "zl", "core"))
    taps = P(None, ("x", "zl", "core"))
    return jax.shard_map(
        on_device,
        mesh=fine,
        in_specs=(signal, signal, signal, signal, taps),
        out_specs=(signal, signal, signal, taps),
        check_vma=False,
    )
```

```python
import math

import jax
import jax.numpy as jnp
import numpy as np
from jax import lax
from jax.experimental import pallas as pl
from jax.experimental.pallas import tpu as pltpu
from jax.sharding import Mesh, PartitionSpec as P

AXES = ("zh", "y", "x", "zl", "core")
ORDERS = ((3, 2, 1, 0), (1, 0, 3, 2))
STEPS = [
    [
        (2 * zh + core, 2 * ORDERS[(step + core + zh) % 2][zh] + 1 - core)
        for zh in range(4)
        for core in range(2)
    ]
    for step in range(2)
]
FAR = ("zl", "x", "y", "core")
BLOCKS = 17
CLASSES = [0, 16, 8, 4, 20] + [8 * j + 2 for j in range(4)] + [4 * j + 1 for j in range(8)]
VMEM = pl.BlockSpec(memory_space=pltpu.VMEM)
HBM = pl.BlockSpec(memory_space=pltpu.HBM)
PARAMS = pltpu.CompilerParams(vmem_limit_bytes=48 * 1024 * 1024)


def tables():
    lane = np.arange(128)
    forward = np.zeros((256, 256))
    angle = 2 * np.pi * np.outer(lane, lane) / 128
    c, s = np.cos(angle), np.sin(angle)
    forward = np.block([[c, -s], [s, c]])
    inverse = np.block([[c, s], [-s, c]]) * (2.0 / 8192)

    def split(table):
        high = table.astype(np.float32).astype(jnp.bfloat16)
        low = (table - high.astype(np.float64)).astype(np.float32).astype(jnp.bfloat16)
        return np.concatenate([high, low], 0)

    row_half = np.arange(8) // 4
    twiddle = np.zeros((BLOCKS, 2, 8, 128), np.float32)
    rowfix = np.zeros((BLOCKS, 2, 8, 128), np.float32)
    for index, k in enumerate(CLASSES):
        angle = -2 * np.pi * np.outer(k + 32 * row_half, lane) / 8192
        twiddle[index, 0], twiddle[index, 1] = np.cos(angle), np.sin(angle)
        angle = np.repeat((-2 * np.pi * k * row_half / 64)[:, None], 128, 1)
        rowfix[index, 0], rowfix[index, 1] = np.cos(angle), np.sin(angle)
    return split(forward), split(inverse), twiddle, rowfix


def add(a, b):
    return (a[0] + b[0], a[1] + b[1])


def sub(a, b):
    return (a[0] - b[0], a[1] - b[1])


def turn(a, step, period, sign):
    step = step % period
    if step == 0:
        return a
    if 4 * step == period:
        return (-a[1], a[0]) if sign > 0 else (a[1], -a[0])
    if 8 * step == period:
        r = np.float32(math.sqrt(0.5))
        if sign > 0:
            return ((a[0] - a[1]) * r, (a[0] + a[1]) * r)
        return ((a[0] + a[1]) * r, (a[1] - a[0]) * r)
    angle = sign * 2 * math.pi * step / period
    c, s = np.float32(math.cos(angle)), np.float32(math.sin(angle))
    return (a[0] * c - a[1] * s, a[0] * s + a[1] * c)


def small_dft(z, sign):
    n = len(z)
    if n == 1:
        return z
    even, odd = small_dft(z[0::2], sign), small_dft(z[1::2], sign)
    odd = [turn(value, j, n, sign) for j, value in enumerate(odd)]
    return [add(a, b) for a, b in zip(even, odd)] + [sub(a, b) for a, b in zip(even, odd)]


def blocks_forward(x):
    v = [x[c] + x[c + 8] for c in range(8)]
    u = [x[c] - x[c + 8] for c in range(8)]
    odd = small_dft([turn((x[c], -x[c + 8]), c, 32, -1) for c in range(8)], -1)
    two = small_dft([turn((u[c], -u[c + 4]), c, 16, -1) for c in range(4)], -1)
    a = [v[c] + v[c + 4] for c in range(4)]
    b = [v[c] - v[c + 4] for c in range(4)]
    four = small_dft([turn((b[c], -b[c + 2]), c, 8, -1) for c in range(2)], -1)
    e, o = a[0] + a[2], a[1] + a[3]
    eight = (a[0] - a[2], a[3] - a[1])
    return [(e + o, None), (e - o, None), eight] + four + two + odd


def blocks_inverse(spectrum):
    zero, sixteen, eight = spectrum[0], spectrum[1], spectrum[2]
    four, two, odd = spectrum[3:5], spectrum[5:9], spectrum[9:17]
    e, o = (zero[0] + sixteen[0]) * 0.5, (zero[0] - sixteen[0]) * 0.5
    a = [e + eight[0], o - eight[1], e - eight[0], o + eight[1]]
    g = [turn(value, c, 8, 1) for c, value in enumerate(small_dft(four, 1))]
    b = [g[0][0], g[1][0], -g[0][1], -g[1][1]]
    v = [a[c] + b[c] for c in range(4)] + [a[c] - b[c] for c in range(4)]
    g = [turn(value, c, 16, 1) for c, value in enumerate(small_dft(two, 1))]
    u = [value[0] for value in g] + [-value[1] for value in g]
    g = [turn(value, c, 32, 1) for c, value in enumerate(small_dft(odd, 1))]
    p = [v[c] + u[c] for c in range(8)]
    m = [v[c] - u[c] for c in range(8)]
    return [p[c] + g[c][0] for c in range(8)] + [m[c] - g[c][1] for c in range(8)]


def half_sign():
    rows = lax.broadcasted_iota(jnp.int32, (8, 128), 0)
    return jnp.where(rows < 4, 1.0, -1.0).astype(jnp.float32)


def swap_halves(a):
    return pltpu.roll(a, 4, 0)


def times(a, b, conjugate=False):
    if conjugate:
        return (a[0] * b[0] + a[1] * b[1], a[1] * b[0] - a[0] * b[1])
    return (a[0] * b[0] - a[1] * b[1], a[0] * b[1] + a[1] * b[0])


def butterfly(a, sign):
    return (a[0] * sign + swap_halves(a[0]), a[1] * sign + swap_halves(a[1]))


def multiply(source, target, table, start):
    high_table, low_table = table[0:256, :], table[256:512, :]
    block = source[start : start + 136, :]
    high = block.astype(jnp.bfloat16)
    low = (block - high.astype(jnp.float32)).astype(jnp.bfloat16)
    total = jnp.dot(high, low_table, preferred_element_type=jnp.float32)
    total += jnp.dot(low, high_table, preferred_element_type=jnp.float32)
    total += jnp.dot(high, high_table, preferred_element_type=jnp.float32)
    target[start : start + 136, :] = total


def channel_bases():
    odd = lax.axis_index("zh") % 2
    return odd * 64, (1 - odd) * 64


def pack_kernel(value_hbm, key_hbm, query_hbm, cot_hbm, filter_hbm, out_ref, value_ref, key_ref, cot_ref, query_ref, filter_ref, sems):
    copies = [
        pltpu.make_async_copy(value_hbm, value_ref, sems.at[0]),
        pltpu.make_async_copy(key_hbm, key_ref, sems.at[1]),
        pltpu.make_async_copy(cot_hbm, cot_ref, sems.at[2]),
        pltpu.make_async_copy(query_hbm, query_ref, sems.at[3]),
    ]
    for copy in copies:
        copy.start()
    y, bases = lax.axis_index("y"), channel_bases()
    lanes = pl.ds(pl.multiple_of((y // 2) * 128, 128), 128)
    for core in range(2):
        rows = pl.ds(pl.multiple_of(bases[core] + (y % 2) * 32, 32), 32)
        copies.append(pltpu.make_async_copy(filter_hbm.at[rows, lanes], filter_ref.at[core], sems.at[4 + core]))
        copies[-1].start()
    places = [
        (core * 9 + half * 4 + j, pl.ds(pl.multiple_of(bases[core] + j * 32, 32), 32), pl.ds(half * 128, 128))
        for core in range(2)
        for j in range(2)
        for half in range(2)
    ]
    copies[0].wait()
    copies[1].wait()
    for at, rows, lanes in places:
        out_ref[pl.ds(at, 32, stride=18), :] = key_ref[rows, lanes] * value_ref[rows, lanes]
    copies[2].wait()
    copies[3].wait()
    for at, rows, lanes in places:
        out_ref[pl.ds(at + 2, 32, stride=18), :] = cot_ref[rows, lanes] * query_ref[rows, lanes]
    for core in range(2):
        copies[4 + core].wait()
        out_ref[pl.ds(core * 9 + 8, 32, stride=18), :] = filter_ref[core] * (1.0 / 64)


def place(y, c):
    return (c // 2 % 2) * 32 + (c // 4) * 8 + y * 2 + c % 2


def spectrum_rows(blocks, scratch, base, sign, twiddle_ref, rowfix_ref):
    for index, value in enumerate(blocks_forward(blocks)):
        fix = (rowfix_ref[index, 0], rowfix_ref[index, 1])
        if value[1] is None:
            value = (value[0] * fix[0], value[0] * fix[1])
        else:
            value = times(value, fix)
        value = butterfly(value, sign)
        value = times(value, (twiddle_ref[index, 0], twiddle_ref[index, 1]))
        at = base + index * 8
        scratch[at : at + 8, 0:128] = value[0]
        scratch[at : at + 8, 128:256] = value[1]


def blocks_of(scratch, base, sign, twiddle_ref, rowfix_ref):
    spectrum = []
    for index in range(BLOCKS):
        at = base + index * 8
        value = (scratch[at : at + 8, 0:128], scratch[at : at + 8, 128:256])
        value = times(value, (twiddle_ref[index, 0], twiddle_ref[index, 1]), True)
        value = butterfly(value, sign)
        spectrum.append(times(value, (rowfix_ref[index, 0], rowfix_ref[index, 1]), True))
    return blocks_inverse(spectrum)


def forward_kernel(signal_ref, forward_ref, inverse_ref, twiddle_ref, rowfix_ref, spec_ref, part_ref, raw):
    sign = half_sign()
    for y in range(4):
        blocks = [signal_ref[place(y, c) * 9 : place(y, c) * 9 + 8, :] for c in range(16)]
        spectrum_rows(blocks, raw, y * 136, sign, twiddle_ref, rowfix_ref)
        multiply(raw, spec_ref, forward_ref, y * 136)
    for index in range(BLOCKS):
        total = None
        for y in range(4):
            at = y * 136 + index * 8
            value = (spec_ref[at : at + 8, 0:128], spec_ref[at : at + 8, 128:256])
            weight = (pltpu.roll(value[0], 6, 0), pltpu.roll(value[1], 6, 0))
            term = times(weight, value, True)
            total = term if total is None else add(total, term)
        raw[544 + index * 8 : 552 + index * 8, 0:128] = total[0]
        raw[544 + index * 8 : 552 + index * 8, 128:256] = total[1]
    multiply(raw, raw, inverse_ref, 544)
    blocks = blocks_of(raw, 544, sign, twiddle_ref, rowfix_ref)
    for c in range(16):
        for half in range(2):
            at = c * 4 + half * 2
            part_ref[at : at + 2, :] = blocks[c][half * 4 : half * 4 + 2, :]


def inverse_kernel(signal_ref, spec_ref, forward_ref, inverse_ref, twiddle_ref, rowfix_ref, out_ref, raw, spec, taps):
    sign = half_sign()
    for y in range(4):
        at = (y // 2) * 4 + y % 2
        for c in range(4):
            rows = signal_ref[pl.ds(place(y, c) * 9 + 8, 4, stride=72), :]
            taps[pl.ds(c * 8 + at, 4, stride=32), :] = rows
            taps[pl.ds(c * 8 + at + 2, 4, stride=32), :] = rows
    spectrum_rows([taps[c * 8 : c * 8 + 8, :] for c in range(16)], raw, 544, sign, twiddle_ref, rowfix_ref)
    multiply(raw, spec, forward_ref, 544)
    rows = lax.broadcasted_iota(jnp.int32, (8, 128), 0)
    flip = jnp.where(rows % 4 < 2, 1.0, -1.0).astype(jnp.float32)
    for y in range(4):
        for index in range(BLOCKS):
            at = 544 + index * 8
            tap = (spec[at : at + 8, 0:128], spec[at : at + 8, 128:256] * flip)
            at = y * 136 + index * 8
            value = times((spec_ref[at : at + 8, 0:128], spec_ref[at : at + 8, 128:256]), tap)
            raw[at : at + 8, 0:128] = value[0]
            raw[at : at + 8, 128:256] = value[1]
        multiply(raw, spec, inverse_ref, y * 136)
        blocks = blocks_of(spec, y * 136, sign, twiddle_ref, rowfix_ref)
        for c in range(16):
            at = place(y, c) * 12
            out_ref[at : at + 8, :] = blocks[c]


def filter_kernel(part_ref, *refs):
    *more_refs, message_ref, out_ref = refs
    out_ref[...] = message_ref[...]
    for c in range(0, 16, 2):
        pair = part_ref[c * 4 : c * 4 + 8, :]
        for more in more_refs:
            pair = pair + more[c * 4 : c * 4 + 8, :]
        pair = pair * (1.0 / 64)
        for y in range(4):
            at = place(y, c) * 12
            out_ref[at + 8 : at + 12, :] = pair[0:4, :]
            out_ref[at + 20 : at + 24, :] = pair[4:8, :]


def unpack_kernel(signal_ref, value_ref, key_ref, cot_ref, query_out, key_out, value_out, filter_out):
    bases = channel_bases()
    for core in range(2):
        for j in range(2):
            rows = pl.ds(pl.multiple_of(bases[core] + j * 32, 32), 32)
            for half in range(2):
                lanes = pl.ds(half * 128, 128)
                at = core * 12 + half * 4 + j
                conv = signal_ref[pl.ds(at, 32, stride=24), :]
                grad = signal_ref[pl.ds(at + 2, 32, stride=24), :]
                query_out[rows, lanes] = cot_ref[rows, lanes] * conv
                key_out[rows, lanes] = grad * value_ref[rows, lanes]
                value_out[rows, lanes] = grad * key_ref[rows, lanes]
                filter_out[rows, lanes] = signal_ref[pl.ds(core * 12 + 8 + half * 2 + j, 32, stride=24), :]


def call(kernel, shapes, inputs, scratch=(), copies=0, **extra):
    return pl.pallas_call(
        kernel,
        out_shape=[jax.ShapeDtypeStruct(shape, jnp.float32) for shape in shapes],
        in_specs=[HBM if copies else VMEM] * inputs,
        out_specs=[VMEM] * len(shapes),
        scratch_shapes=[pltpu.VMEM(shape, jnp.float32) for shape in scratch]
        + ([pltpu.SemaphoreType.DMA((copies,))] if copies else []),
        compiler_params=PARAMS,
        **extra,
    )


def exchange(array, axes):
    return lax.all_to_all(array, axes, split_axis=0, concat_axis=0, tiled=True)


def on_device(value_in, key_in, query_in, cotangent, filter_param):
    value_in, key_in, query_in, cotangent = value_in[0], key_in[0], query_in[0], cotangent[0]
    forward, inverse, twiddle, rowfix = [jnp.asarray(table) for table in tables()]
    pinned = [pltpu.with_memory_space_constraint(a, pltpu.HBM) for a in (value_in, key_in, query_in, cotangent, filter_param)]
    shape = (128, 256)
    message, value, key, cot = call(pack_kernel, [(576, 128)] + [shape] * 3, 5, [shape, (2, 32, 128)], copies=6)(*pinned)
    signal = exchange(message.reshape(64, 1, 1152), FAR).reshape(576, 128)
    spec, part = call(forward_kernel, [(544, 256), (64, 128)], 5, [(680, 256)])(
        signal, forward, inverse, twiddle, rowfix
    )
    for pairs in STEPS:
        part = part + lax.ppermute(part, ("zh", "core"), pairs)
    (message,) = call(inverse_kernel, [(768, 128)], 6, [(680, 256)] * 2 + [(128, 128)])(
        signal, spec, forward, inverse, twiddle, rowfix
    )
    (message,) = call(filter_kernel, [(768, 128)], 2)(part, message)
    signal = exchange(message.reshape(64, 1, 1536), FAR).reshape(768, 128)
    query_grad, key_grad, value_grad, filter_grad = call(unpack_kernel, [shape] * 4, 4)(signal, value, key, cot)
    return query_grad[None], key_grad[None], value_grad[None], filter_grad


def solution(mesh):
    fine = Mesh(mesh.devices.reshape(4, 4, 4, 2, 2), AXES)
    signal = P(("zh", "y"), None, ("x", "zl", "core"))
    taps = P(None, ("x", "zl", "core"))
    return jax.shard_map(
        on_device,
        mesh=fine,
        in_specs=(signal, signal, signal, signal, taps),
        out_specs=(signal, signal, signal, taps),
        check_vma=False,
    )
```

```python
import math

import jax
import jax.numpy as jnp
import numpy as np
from jax import lax
from jax.experimental import pallas as pl
from jax.experimental.pallas import tpu as pltpu
from jax.sharding import Mesh, PartitionSpec as P

AXES = ("zh", "y", "x", "zl", "core")
ORDERS = ((3, 2, 1, 0), (1, 0, 3, 2))
STEPS = [
    [
        (2 * zh + core, 2 * ORDERS[(step + core + zh) % 2][zh] + 1 - core)
        for zh in range(4)
        for core in range(2)
    ]
    for step in range(2)
]
FAR = ("zl", "x", "y", "core")
BLOCKS = 17
CLASSES = [0, 16, 8, 4, 20] + [8 * j + 2 for j in range(4)] + [4 * j + 1 for j in range(8)]
VMEM = pl.BlockSpec(memory_space=pltpu.VMEM)
HBM = pl.BlockSpec(memory_space=pltpu.HBM)
PARAMS = pltpu.CompilerParams(vmem_limit_bytes=48 * 1024 * 1024)


def tables():
    lane = np.arange(128)
    forward = np.zeros((256, 256))
    angle = 2 * np.pi * np.outer(lane, lane) / 128
    c, s = np.cos(angle), np.sin(angle)
    forward = np.block([[c, -s], [s, c]])
    inverse = np.block([[c, s], [-s, c]]) * (2.0 / 8192)

    def split(table):
        high = table.astype(np.float32).astype(jnp.bfloat16)
        low = (table - high.astype(np.float64)).astype(np.float32).astype(jnp.bfloat16)
        return np.concatenate([high, high, low], 0)

    row_half = np.arange(8) // 4
    twiddle = np.zeros((BLOCKS, 2, 8, 128), np.float32)
    rowfix = np.zeros((BLOCKS, 2, 8, 128), np.float32)
    for index, k in enumerate(CLASSES):
        angle = -2 * np.pi * np.outer(k + 32 * row_half, lane) / 8192
        twiddle[index, 0], twiddle[index, 1] = np.cos(angle), np.sin(angle)
        angle = np.repeat((-2 * np.pi * k * row_half / 64)[:, None], 128, 1)
        rowfix[index, 0], rowfix[index, 1] = np.cos(angle), np.sin(angle)
    return split(forward), split(inverse), twiddle, rowfix


def add(a, b):
    return (a[0] + b[0], a[1] + b[1])


def sub(a, b):
    return (a[0] - b[0], a[1] - b[1])


def turn(a, step, period, sign):
    step = step % period
    if step == 0:
        return a
    if 4 * step == period:
        return (-a[1], a[0]) if sign > 0 else (a[1], -a[0])
    if 8 * step == period:
        r = np.float32(math.sqrt(0.5))
        if sign > 0:
            return ((a[0] - a[1]) * r, (a[0] + a[1]) * r)
        return ((a[0] + a[1]) * r, (a[1] - a[0]) * r)
    angle = sign * 2 * math.pi * step / period
    c, s = np.float32(math.cos(angle)), np.float32(math.sin(angle))
    return (a[0] * c - a[1] * s, a[0] * s + a[1] * c)


def small_dft(z, sign):
    n = len(z)
    if n == 1:
        return z
    even, odd = small_dft(z[0::2], sign), small_dft(z[1::2], sign)
    odd = [turn(value, j, n, sign) for j, value in enumerate(odd)]
    return [add(a, b) for a, b in zip(even, odd)] + [sub(a, b) for a, b in zip(even, odd)]


def blocks_forward(x):
    v = [x[c] + x[c + 8] for c in range(8)]
    u = [x[c] - x[c + 8] for c in range(8)]
    odd = small_dft([turn((x[c], -x[c + 8]), c, 32, -1) for c in range(8)], -1)
    two = small_dft([turn((u[c], -u[c + 4]), c, 16, -1) for c in range(4)], -1)
    a = [v[c] + v[c + 4] for c in range(4)]
    b = [v[c] - v[c + 4] for c in range(4)]
    four = small_dft([turn((b[c], -b[c + 2]), c, 8, -1) for c in range(2)], -1)
    e, o = a[0] + a[2], a[1] + a[3]
    eight = (a[0] - a[2], a[3] - a[1])
    return [(e + o, None), (e - o, None), eight] + four + two + odd


def blocks_inverse(spectrum):
    zero, sixteen, eight = spectrum[0], spectrum[1], spectrum[2]
    four, two, odd = spectrum[3:5], spectrum[5:9], spectrum[9:17]
    e, o = (zero[0] + sixteen[0]) * 0.5, (zero[0] - sixteen[0]) * 0.5
    a = [e + eight[0], o - eight[1], e - eight[0], o + eight[1]]
    g = [turn(value, c, 8, 1) for c, value in enumerate(small_dft(four, 1))]
    b = [g[0][0], g[1][0], -g[0][1], -g[1][1]]
    v = [a[c] + b[c] for c in range(4)] + [a[c] - b[c] for c in range(4)]
    g = [turn(value, c, 16, 1) for c, value in enumerate(small_dft(two, 1))]
    u = [value[0] for value in g] + [-value[1] for value in g]
    g = [turn(value, c, 32, 1) for c, value in enumerate(small_dft(odd, 1))]
    p = [v[c] + u[c] for c in range(8)]
    m = [v[c] - u[c] for c in range(8)]
    return [p[c] + g[c][0] for c in range(8)] + [m[c] - g[c][1] for c in range(8)]


def half_sign():
    rows = lax.broadcasted_iota(jnp.int32, (8, 128), 0)
    return jnp.where(rows < 4, 1.0, -1.0).astype(jnp.float32)


def swap_halves(a):
    return pltpu.roll(a, 4, 0)


def times(a, b, conjugate=False):
    if conjugate:
        return (a[0] * b[0] + a[1] * b[1], a[1] * b[0] - a[0] * b[1])
    return (a[0] * b[0] - a[1] * b[1], a[0] * b[1] + a[1] * b[0])


def butterfly(a, sign):
    return (a[0] * sign + swap_halves(a[0]), a[1] * sign + swap_halves(a[1]))


def multiply(source, target, table, start):
    block = source[start : start + 136, :]
    high = block.astype(jnp.bfloat16)
    low = (block - high.astype(jnp.float32)).astype(jnp.bfloat16)
    parts = jnp.concatenate([high, low, high], 1)
    target[start : start + 136, :] = jnp.dot(parts, table[...], preferred_element_type=jnp.float32)


def channel_bases():
    odd = lax.axis_index("zh") % 2
    return odd * 64, (1 - odd) * 64


def pack_kernel(value_hbm, key_hbm, query_hbm, cot_hbm, filter_hbm, out_ref, value_ref, key_ref, cot_ref, query_ref, filter_ref, sems):
    copies = [
        pltpu.make_async_copy(value_hbm, value_ref, sems.at[0]),
        pltpu.make_async_copy(key_hbm, key_ref, sems.at[1]),
        pltpu.make_async_copy(cot_hbm, cot_ref, sems.at[2]),
        pltpu.make_async_copy(query_hbm, query_ref, sems.at[3]),
    ]
    for copy in copies:
        copy.start()
    y, bases = lax.axis_index("y"), channel_bases()
    lanes = pl.ds(pl.multiple_of((y // 2) * 128, 128), 128)
    for core in range(2):
        rows = pl.ds(pl.multiple_of(bases[core] + (y % 2) * 32, 32), 32)
        copies.append(pltpu.make_async_copy(filter_hbm.at[rows, lanes], filter_ref.at[core], sems.at[4 + core]))
        copies[-1].start()
    places = [
        (core * 9 + half * 4 + j, pl.ds(pl.multiple_of(bases[core] + j * 32, 32), 32), pl.ds(half * 128, 128))
        for core in range(2)
        for j in range(2)
        for half in range(2)
    ]
    copies[0].wait()
    copies[1].wait()
    for at, rows, lanes in places:
        out_ref[pl.ds(at, 32, stride=18), :] = key_ref[rows, lanes] * value_ref[rows, lanes]
    copies[2].wait()
    copies[3].wait()
    for at, rows, lanes in places:
        out_ref[pl.ds(at + 2, 32, stride=18), :] = cot_ref[rows, lanes] * query_ref[rows, lanes]
    for core in range(2):
        copies[4 + core].wait()
        out_ref[pl.ds(core * 9 + 8, 32, stride=18), :] = filter_ref[core] * (1.0 / 64)


def place(y, c):
    return (c // 2 % 2) * 32 + (c // 4) * 8 + y * 2 + c % 2


def spectrum_rows(blocks, scratch, base, sign, twiddle_ref, rowfix_ref):
    for index, value in enumerate(blocks_forward(blocks)):
        fix = (rowfix_ref[index, 0], rowfix_ref[index, 1])
        if value[1] is None:
            value = (value[0] * fix[0], value[0] * fix[1])
        else:
            value = times(value, fix)
        value = butterfly(value, sign)
        value = times(value, (twiddle_ref[index, 0], twiddle_ref[index, 1]))
        at = base + index * 8
        scratch[at : at + 8, 0:128] = value[0]
        scratch[at : at + 8, 128:256] = value[1]


def blocks_of(scratch, base, sign, twiddle_ref, rowfix_ref):
    spectrum = []
    for index in range(BLOCKS):
        at = base + index * 8
        value = (scratch[at : at + 8, 0:128], scratch[at : at + 8, 128:256])
        value = times(value, (twiddle_ref[index, 0], twiddle_ref[index, 1]), True)
        value = butterfly(value, sign)
        spectrum.append(times(value, (rowfix_ref[index, 0], rowfix_ref[index, 1]), True))
    return blocks_inverse(spectrum)


def forward_kernel(signal_ref, forward_ref, inverse_ref, twiddle_ref, rowfix_ref, spec_ref, part_ref, raw):
    sign = half_sign()
    for y in range(4):
        blocks = [signal_ref[place(y, c) * 9 : place(y, c) * 9 + 8, :] for c in range(16)]
        spectrum_rows(blocks, raw, y * 136, sign, twiddle_ref, rowfix_ref)
        multiply(raw, spec_ref, forward_ref, y * 136)
    for index in range(BLOCKS):
        total = None
        for y in range(4):
            at = y * 136 + index * 8
            value = (spec_ref[at : at + 8, 0:128], spec_ref[at : at + 8, 128:256])
            weight = (pltpu.roll(value[0], 6, 0), pltpu.roll(value[1], 6, 0))
            term = times(weight, value, True)
            total = term if total is None else add(total, term)
        raw[544 + index * 8 : 552 + index * 8, 0:128] = total[0]
        raw[544 + index * 8 : 552 + index * 8, 128:256] = total[1]
    multiply(raw, raw, inverse_ref, 544)
    blocks = blocks_of(raw, 544, sign, twiddle_ref, rowfix_ref)
    for c in range(16):
        for half in range(2):
            at = c * 4 + half * 2
            part_ref[at : at + 2, :] = blocks[c][half * 4 : half * 4 + 2, :]


def inverse_kernel(signal_ref, spec_ref, forward_ref, inverse_ref, twiddle_ref, rowfix_ref, out_ref, raw, spec, taps):
    sign = half_sign()
    for y in range(4):
        at = (y // 2) * 4 + y % 2
        for c in range(4):
            rows = signal_ref[pl.ds(place(y, c) * 9 + 8, 4, stride=72), :]
            taps[pl.ds(c * 8 + at, 4, stride=32), :] = rows
            taps[pl.ds(c * 8 + at + 2, 4, stride=32), :] = rows
    spectrum_rows([taps[c * 8 : c * 8 + 8, :] for c in range(16)], raw, 544, sign, twiddle_ref, rowfix_ref)
    multiply(raw, spec, forward_ref, 544)
    rows = lax.broadcasted_iota(jnp.int32, (8, 128), 0)
    flip = jnp.where(rows % 4 < 2, 1.0, -1.0).astype(jnp.float32)
    for y in range(4):
        for index in range(BLOCKS):
            at = 544 + index * 8
            tap = (spec[at : at + 8, 0:128], spec[at : at + 8, 128:256] * flip)
            at = y * 136 + index * 8
            value = times((spec_ref[at : at + 8, 0:128], spec_ref[at : at + 8, 128:256]), tap)
            raw[at : at + 8, 0:128] = value[0]
            raw[at : at + 8, 128:256] = value[1]
        multiply(raw, spec, inverse_ref, y * 136)
        blocks = blocks_of(spec, y * 136, sign, twiddle_ref, rowfix_ref)
        for c in range(16):
            at = place(y, c) * 12
            out_ref[at : at + 8, :] = blocks[c]


def filter_kernel(part_ref, *refs):
    *more_refs, message_ref, out_ref = refs
    out_ref[...] = message_ref[...]
    for c in range(0, 16, 2):
        pair = part_ref[c * 4 : c * 4 + 8, :]
        for more in more_refs:
            pair = pair + more[c * 4 : c * 4 + 8, :]
        pair = pair * (1.0 / 64)
        for y in range(4):
            at = place(y, c) * 12
            out_ref[at + 8 : at + 12, :] = pair[0:4, :]
            out_ref[at + 20 : at + 24, :] = pair[4:8, :]


def unpack_kernel(signal_ref, value_ref, key_ref, cot_ref, query_out, key_out, value_out, filter_out):
    bases = channel_bases()
    for core in range(2):
        for j in range(2):
            rows = pl.ds(pl.multiple_of(bases[core] + j * 32, 32), 32)
            for half in range(2):
                lanes = pl.ds(half * 128, 128)
                at = core * 12 + half * 4 + j
                conv = signal_ref[pl.ds(at, 32, stride=24), :]
                grad = signal_ref[pl.ds(at + 2, 32, stride=24), :]
                query_out[rows, lanes] = cot_ref[rows, lanes] * conv
                key_out[rows, lanes] = grad * value_ref[rows, lanes]
                value_out[rows, lanes] = grad * key_ref[rows, lanes]
                filter_out[rows, lanes] = signal_ref[pl.ds(core * 12 + 8 + half * 2 + j, 32, stride=24), :]


def call(kernel, shapes, inputs, scratch=(), copies=0, **extra):
    return pl.pallas_call(
        kernel,
        out_shape=[jax.ShapeDtypeStruct(shape, jnp.float32) for shape in shapes],
        in_specs=[HBM if copies else VMEM] * inputs,
        out_specs=[VMEM] * len(shapes),
        scratch_shapes=[pltpu.VMEM(shape, jnp.float32) for shape in scratch]
        + ([pltpu.SemaphoreType.DMA((copies,))] if copies else []),
        compiler_params=PARAMS,
        **extra,
    )


def exchange(array, axes):
    return lax.all_to_all(array, axes, split_axis=0, concat_axis=0, tiled=True)


def on_device(value_in, key_in, query_in, cotangent, filter_param):
    value_in, key_in, query_in, cotangent = value_in[0], key_in[0], query_in[0], cotangent[0]
    forward, inverse, twiddle, rowfix = [jnp.asarray(table) for table in tables()]
    pinned = [pltpu.with_memory_space_constraint(a, pltpu.HBM) for a in (value_in, key_in, query_in, cotangent, filter_param)]
    shape = (128, 256)
    message, value, key, cot = call(pack_kernel, [(576, 128)] + [shape] * 3, 5, [shape, (2, 32, 128)], copies=6)(*pinned)
    signal = exchange(message.reshape(64, 1, 1152), FAR).reshape(576, 128)
    spec, part = call(forward_kernel, [(544, 256), (64, 128)], 5, [(680, 256)])(
        signal, forward, inverse, twiddle, rowfix
    )
    part = part + lax.ppermute(part, ("zh", "core"), STEPS[0])
    more = lax.ppermute(part, ("zh", "core"), STEPS[1])
    (message,) = call(inverse_kernel, [(768, 128)], 6, [(680, 256)] * 2 + [(128, 128)])(
        signal, spec, forward, inverse, twiddle, rowfix
    )
    (message,) = call(filter_kernel, [(768, 128)], 3)(part, more, message)
    signal = exchange(message.reshape(64, 1, 1536), FAR).reshape(768, 128)
    query_grad, key_grad, value_grad, filter_grad = call(unpack_kernel, [shape] * 4, 4)(signal, value, key, cot)
    return query_grad[None], key_grad[None], value_grad[None], filter_grad


def solution(mesh):
    fine = Mesh(mesh.devices.reshape(4, 4, 4, 2, 2), AXES)
    signal = P(("zh", "y"), None, ("x", "zl", "core"))
    taps = P(None, ("x", "zl", "core"))
    return jax.shard_map(
        on_device,
        mesh=fine,
        in_specs=(signal, signal, signal, signal, taps),
        out_specs=(signal, signal, signal, taps),
        check_vma=False,
    )
```
